256 devices in a mesh: row: 32 (over y, x, core), col: 8 (over z).
Axes of the slice: x: 4, y: 4, z: 8, core: 2. Of those that a mesh axis runs over, the one named last changes fastest.
Arguments:
- panel: float32 [4, 4096, 256], P(None, 'row'), may hold values from -1.5 to 1.5, as said below
- matrix: float32 [4, 4096, 16, 1024], P(None, 'row', None, 'col'), may hold values from -40 to 40, as said below
Outputs:
- factor: float32 [256, 256], replicated
- updated: float32 [4, 4096, 16, 1024], P(None, 'row', None, 'col')
The draws below stay inside these ranges and needn't reach their ends.
Inputs may be any that keep to these rules, and one draw needn't show every extreme that they name: matrix, read as an 16384 x 16384 matrix, is exactly symmetric. panel has full column rank.
All inputs are finite; a program needn't handle non-finite values.
Results may differ from the reference program's by a relative error of at most 0.000061.
Values sent between devices are 32-bit elements; how exact they have to be, the bound alone decides.
A program may use at most 64 MiB of HBM per device.

```python
import math
import jax
import jax.numpy as jnp
from jax import lax

PANEL = 256
ROW_CYCLES = 4
COL_CYCLES = 16
ORDER = 16384


def draw_panel(key, part):
    key = jax.random.fold_in(key, 11)
    span = ORDER // ROW_CYCLES
    ramp = 3.0 ** (jnp.arange(span, dtype=jnp.float32) / span)
    base = jnp.clip(jax.random.normal(key, (ROW_CYCLES, span, PANEL), jnp.float32), -4.0, 4.0)
    return base * ramp[None, :, None] * ORDER ** (-0.5)


def draw_matrix(key, part):
    key = jax.random.fold_in(key, 23)
    base = jax.random.normal(key, (ORDER, ORDER), jnp.float32)
    sym = (base + base.T) * math.sqrt(0.5)
    return sym.reshape(ROW_CYCLES, ORDER // ROW_CYCLES, COL_CYCLES, ORDER // COL_CYCLES)


def setup_inputs(seed: int = 0) -> dict:
    key_of = jax.random.split(jax.random.key(seed), 3)
    panel = draw_panel(jax.random.fold_in(key_of[2], 71), 0)
    matrix = draw_matrix(jax.random.fold_in(key_of[2], 71), 0)
    return dict(panel=panel, matrix=matrix)


def reference(panel, matrix):
    highest = lax.Precision.HIGHEST
    whole_panel = panel.reshape(ORDER, PANEL)
    whole = matrix.reshape(ORDER, ORDER)
    gram = jnp.dot(whole_panel.T, whole_panel, precision=highest)
    lower = jnp.linalg.cholesky(gram)
    basis = jax.scipy.linalg.solve_triangular(lower, whole_panel.T, lower=True).T
    image = jnp.dot(whole, basis, precision=highest)
    curvature = jnp.dot(basis.T, image, precision=highest)
    wing = 2.0 * image - 2.0 * jnp.dot(basis, curvature, precision=highest)
    result = whole - jnp.dot(basis, wing.T, precision=highest) - jnp.dot(wing, basis.T, precision=highest)
    return (lower.T, result.reshape(matrix.shape))
```

```python
import functools

import jax
import jax.numpy as jnp
from jax import lax
from jax.experimental import pallas as pl
from jax.experimental.pallas import tpu as pltpu
from jax.sharding import PartitionSpec as P

MESH = pl.DeviceIdType.MESH
HIGHEST = lax.Precision.HIGHEST
F32 = jnp.float32
BF16 = jnp.bfloat16
W = 256
ROWS = 512
CHUNK = 64
NCH = 4
NB = 32


def remote(src, dst, send, recv, row, col):
    return pltpu.make_async_remote_copy(
        src_ref=src, dst_ref=dst, send_sem=send, recv_sem=recv,
        device_id={"row": row, "col": col}, device_id_type=MESH)


def split(x):
    hi = x.astype(BF16)
    return hi, (x - hi.astype(F32)).astype(BF16)


NN = (((1,), (0,)), ((), ()))
NT = (((1,), (1,)), ((), ()))
TN = (((0,), (0,)), ((), ()))


def dot(a, b, dims=NN, precision=None):
    return lax.dot_general(a, b, dims, precision=precision, preferred_element_type=F32)


def dot3(a, b, dims=NN):
    ah, al = split(a)
    bh, bl = split(b)
    return dot(ah, bh, dims) + (dot(ah, bl, dims) + dot(al, bh, dims))


def factorize(gram, work):
    lane = lax.broadcasted_iota(jnp.int32, (NB, 128), 1)
    sub = lax.broadcasted_iota(jnp.int32, (NB, 128), 0)
    eye = (lane == sub).astype(F32)
    for b in range(W // NB):
        lo = b * NB
        left = gram[lo:lo + NB, :]
        unit = (lax.broadcasted_iota(jnp.int32, (NB, W), 1) ==
                lax.broadcasted_iota(jnp.int32, (NB, W), 0) + lo).astype(F32)
        rows = jnp.concatenate([left, unit], axis=1)
        if b:
            rows = rows - dot(work[0:lo, lo:lo + NB], work[0:lo, :], TN, HIGHEST)
        tile = jnp.concatenate([rows[:, lo:lo + NB], eye[:, :NB], jnp.zeros((NB, 128 - 2 * NB), F32)], axis=1)
        for i in range(NB):
            row = tile[i:i + 1, :]
            factor = tile[:, i:i + 1] * (1.0 / tile[i:i + 1, i:i + 1])
            tile = jnp.where(sub > i, tile - factor * row, tile)
        pivots = jnp.sum(jnp.where(lane == sub, tile, 0.0), axis=1, keepdims=True)
        inverse = tile[:, NB:2 * NB] * lax.rsqrt(pivots)
        work[lo:lo + NB, :] = dot(inverse, rows, NN, HIGHEST)


def body(panel, a_hbm, factor_out, out_hbm,
         abuf, ahi, alo, pc, yc, chi, clo, part, yrow, rsbuf, gpart, gsum, grs, spart, ssum, srs, work, lhs,
         a_sem, o_sem, px, py, ps, p0, yx, yy, ys, y0, gr, ga, gs, sr, sa, ss, rr, ra):
    r = lax.axis_index("row")
    c = lax.axis_index("col")
    core = r % 2
    x = (r // 2) % 4
    y = r // 8
    sib = r + 1 - 2 * core
    step = 1 + 2 * core

    def at_row(xx, yy_):
        return (yy_ * 4 + xx) * 2 + core

    xdst = at_row((x + step) % 4, y)
    ydst = at_row(x, (y + step) % 4)
    source_x = c // 2
    source_core = c % 2
    hop = ((x + 4 - source_x) * step) % 4

    load = pltpu.make_async_copy(a_hbm, abuf, a_sem)
    load.start()

    barrier = pltpu.get_barrier_semaphore()
    for row in (sib, at_row((x + 1) % 4, y), at_row((x + 3) % 4, y), at_row(x, (y + 1) % 4), at_row(x, (y + 3) % 4)):
        pl.semaphore_signal(barrier, inc=1, device_id={"row": row, "col": c}, device_id_type=MESH)
    for p in range(1, 8):
        pl.semaphore_signal(barrier, inc=1, device_id={"row": r, "col": (c + p) % 8}, device_id_type=MESH)
    pl.semaphore_wait(barrier, 12)

    on_source = hop == 0
    is_source = jnp.logical_and(on_source, core == source_core)
    is_second = jnp.logical_and(on_source, core != source_core)

    def gather(src, buf, sx, sy, ss_, s0):
        def piece(q, half, t):
            return buf.at[q, pl.ds(half * (NCH * CHUNK) + t * CHUNK, CHUNK), :]

        @pl.when(is_source)
        def _():
            buf[y] = src[...]
            for t in range(NCH):
                ref = piece(y, 1 - core, t)
                remote(ref, ref, s0.at[0, t], s0.at[1, t], sib, c).start()

        for t in range(NCH):
            ref = piece(y, core, t)
            first = remote(ref, ref, s0.at[0, t], s0.at[1, t], sib, c)
            along = remote(ref, ref, sx.at[0, t], sx.at[1, t], xdst, c)

            @pl.when(is_second)
            def _():
                first.wait_recv()

            @pl.when(hop > 0)
            def _():
                along.wait_recv()

            @pl.when(hop < 3)
            def _():
                along.start()

            remote(ref, ref, sy.at[0, 0, t], sy.at[1, 0, t], ydst, c).start()

            @pl.when(jnp.logical_not(is_second))
            def _():
                remote(ref, ref, ss_.at[0, 0, t], ss_.at[1, 0, t], sib, c).start()

        for s in range(1, 4):
            q = (y + 4 * step - s * step) % 4
            for t in range(NCH):
                ref = piece(q, core, t)
                remote(ref, ref, sy.at[0, s - 1, t], sy.at[1, s - 1, t], ydst, c).wait_recv()
                if s < 3:
                    remote(ref, ref, sy.at[0, s, t], sy.at[1, s, t], ydst, c).start()
                remote(ref, ref, ss_.at[0, s, t], ss_.at[1, s, t], sib, c).start()
        for s in range(4):
            q = (y + s * step) % 4
            for t in range(NCH):
                other = piece(q, 1 - core, t)
                copy = remote(other, other, ss_.at[0, s, t], ss_.at[1, s, t], sib, c)
                if s:
                    copy.wait_recv()
                else:
                    @pl.when(jnp.logical_not(is_source))
                    def _():
                        copy.wait_recv()
        for t in range(NCH):
            ref = piece(y, core, t)

            @pl.when(is_source)
            def _():
                remote(ref, ref, s0.at[0, t], s0.at[1, t], sib, c).wait_send()

            @pl.when(hop < 3)
            def _():
                remote(ref, ref, sx.at[0, t], sx.at[1, t], xdst, c).wait_send()

            for s in range(3):
                remote(ref, ref, sy.at[0, s, t], sy.at[1, s, t], ydst, c).wait_send()
            for s in range(4):
                copy = remote(ref, ref, ss_.at[0, s, t], ss_.at[1, s, t], sib, c)
                if s:
                    copy.wait_send()
                else:
                    @pl.when(jnp.logical_not(is_second))
                    def _():
                        copy.wait_send()

    def scatter_copy(src, dst, sems, rows, p):
        z = (c + p) % 8
        return remote(src.at[pl.ds(z * rows, rows), :], dst.at[p], sems.at[0, p], sems.at[1, p], r, z)

    def spread_copy(ref, base, sems, rows, p):
        z = (c + p) % 8
        piece = ref.at[pl.ds(base + c * rows, rows), :]
        return remote(piece, piece, sems.at[0, p], sems.at[1, p], r, z)

    def spread_wait(ref, base, sems, rows, p):
        z = (c + 8 - p) % 8
        piece = ref.at[pl.ds(base + z * rows, rows), :]
        remote(piece, piece, sems.at[0, p], sems.at[1, p], r, (c + p) % 8).wait_recv()

    def reduce_small(partial, slots, total, s_scatter, s_spread, s_sib):
        for p in range(1, 8):
            scatter_copy(partial, slots, s_scatter, 16, p).start()
        for p in range(1, 8):
            scatter_copy(partial, slots, s_scatter, 16, p).wait_recv()
        value = partial[pl.ds(pl.multiple_of(c * 16, 16), 16), :]
        for p in range(1, 8):
            value = value + slots[p]
        base = core * 128
        total[pl.ds(pl.multiple_of(base + c * 16, 16), 16), :] = value
        for p in range(1, 8):
            spread_copy(total, base, s_spread, 16, p).start()
        for p in range(1, 8):
            spread_wait(total, base, s_spread, 16, p)
        half = total.at[pl.ds(base, 128), :]
        other = total.at[pl.ds(128 - base, 128), :]
        share = remote(half, half, s_sib.at[0], s_sib.at[1], sib, c)
        share.start()
        remote(other, other, s_sib.at[0], s_sib.at[1], sib, c).wait_recv()
        for p in range(1, 8):
            scatter_copy(partial, slots, s_scatter, 16, p).wait_send()
            spread_copy(total, base, s_spread, 16, p).wait_send()
        share.wait_send()

    gather(panel, pc, px, py, ps, p0)

    mine = pl.ds(pl.multiple_of(core * 128, 128), 128)
    gpart[...] = jnp.zeros_like(gpart)

    @pl.loop(0, 4)
    def _(q):
        gpart[...] += dot(pc[q, :, mine], pc[q], TN, HIGHEST)

    reduce_small(gpart, grs, gsum, gr, ga, gs)

    load.wait()
    part[...] = jnp.zeros_like(part)
    for q in range(4):
        for i in range(4):
            h, l = split(abuf[pl.ds(4 * i + q, ROWS, stride=16), :])
            ahi[q, :, i * 128:(i + 1) * 128] = h
            alo[q, :, i * 128:(i + 1) * 128] = l

    @pl.loop(0, 4)
    def _(q):
        h, l = split(pc[q])
        chi[q, :, W:] = h
        clo[q, :, W:] = l
        part[...] += dot(ahi[q], h) + (dot(ahi[q], l) + dot(alo[q], h))

    for p in range(1, 8):
        scatter_copy(part, rsbuf, rr, 64, p).start()
    factorize(gsum, work)
    upper = lax.broadcasted_iota(jnp.int32, (W, W), 1) >= lax.broadcasted_iota(jnp.int32, (W, W), 0)
    factor_out[...] = jnp.where(upper, work[:, :W], 0.0)
    inverse = work[:, W:]
    metric = dot(inverse, inverse, TN, HIGHEST)
    first = 2.0 * dot3(panel[...], metric)
    for p in range(1, 8):
        scatter_copy(part, rsbuf, rr, 64, p).wait_recv()
    own = pl.ds(pl.multiple_of(c * 64, 64), 64)
    value = part[own, :]
    for p in range(1, 8):
        value = value + rsbuf[p]
    yrow[own, :] = value
    for p in range(1, 8):
        spread_copy(yrow, 0, ra, 64, p).start()
    for p in range(1, 8):
        spread_wait(yrow, 0, ra, 64, p)

    gather(yrow, yc, yx, yy, ys, y0)

    spart[...] = jnp.zeros_like(spart)

    @pl.loop(0, 4)
    def _(q):
        h, l = split(yc[q])
        chi[q, :, :W] = h
        clo[q, :, :W] = l
        spart[...] += dot3(pc[q, :, mine], yc[q], TN)

    reduce_small(spart, srs, ssum, sr, sa, ss)

    second = 2.0 * dot3(yrow[...] - dot3(first, ssum[...]), metric)
    lhs[0, :, :W], lhs[1, :, :W] = split(first)
    lhs[0, :, W:], lhs[1, :, W:] = split(second)

    @pl.loop(0, 4)
    def _(m):
        rows = pl.ds(pl.multiple_of(m * 128, 128), 128)
        lh = lhs[0, rows, :]
        ll = lhs[1, rows, :]
        for q in range(4):
            value = dot(lh, chi[q], NT) + (dot(lh, clo[q], NT) + dot(ll, chi[q], NT))
            for i in range(4):
                at = pl.ds(m * 2048 + 4 * i + q, 128, stride=16)
                abuf[at, :] = abuf[at, :] - value[:, i * 128:(i + 1) * 128]
        block = pl.ds(pl.multiple_of(m * 2048, 2048), 2048)
        pltpu.make_async_copy(abuf.at[block, :], out_hbm.at[block, :], o_sem.at[m]).start()

    for p in range(1, 8):
        scatter_copy(part, rsbuf, rr, 64, p).wait_send()
        spread_copy(yrow, 0, ra, 64, p).wait_send()
    for m in range(4):
        block = pl.ds(m * 2048, 2048)
        pltpu.make_async_copy(abuf.at[block, :], out_hbm.at[block, :], o_sem.at[m]).wait()


def shards(panel, matrix):
    vmem = functools.partial(pltpu.VMEM)
    dma = pltpu.SemaphoreType.DMA
    gather_sems = [dma((2, NCH)), dma((2, 3, NCH)), dma((2, 4, NCH)), dma((2, NCH))]
    small_sems = [dma((2, 8)), dma((2, 8)), dma((2,))]
    factor, updated = pl.pallas_call(
        body,
        out_shape=(jax.ShapeDtypeStruct((W, W), F32), jax.ShapeDtypeStruct((ROWS * 16, 128), F32)),
        in_specs=[pl.BlockSpec(memory_space=pltpu.VMEM), pl.BlockSpec(memory_space=pl.ANY)],
        out_specs=(pl.BlockSpec(memory_space=pltpu.VMEM), pl.BlockSpec(memory_space=pl.ANY)),
        scratch_shapes=[
            vmem((ROWS * 16, 128), F32),
            vmem((4, ROWS, 512), BF16), vmem((4, ROWS, 512), BF16),
            vmem((4, ROWS, W), F32), vmem((4, ROWS, W), F32),
            vmem((4, ROWS, 2 * W), BF16), vmem((4, ROWS, 2 * W), BF16),
            vmem((ROWS, W), F32), vmem((ROWS, W), F32), vmem((8, 64, W), F32),
            vmem((128, W), F32), vmem((W, W), F32), vmem((8, 16, W), F32),
            vmem((128, W), F32), vmem((W, W), F32), vmem((8, 16, W), F32),
            vmem((W, 2 * W), F32), vmem((2, ROWS, 2 * W), BF16),
            dma, dma((4,)),
        ] + gather_sems + gather_sems + small_sems + small_sems + [dma((2, 8)), dma((2, 8))],
        compiler_params=pltpu.CompilerParams(
            collective_id=0, has_side_effects=True, vmem_limit_bytes=56 * 2**20),
        cost_estimate=pl.CostEstimate(flops=5 * 10**9, bytes_accessed=9 * 2**20, transcendentals=0),
    )(panel.reshape(ROWS, W), matrix.reshape(ROWS * 16, 128))
    return factor, updated.reshape(matrix.shape)


def solution(mesh):
    in_specs = (P(None, "row", None), P(None, "row", None, "col"))
    out_specs = (P(), P(None, "row", None, "col"))
    return jax.shard_map(shards, mesh=mesh, in_specs=in_specs, out_specs=out_specs, check_vma=False)
```

```python
import jax
import jax.numpy as jnp
from jax import lax
from jax.experimental import pallas as pl
from jax.experimental.pallas import tpu as pltpu
from jax.sharding import PartitionSpec as P

MESH = pl.DeviceIdType.MESH
HIGHEST = lax.Precision.HIGHEST
F32 = jnp.float32
BF16 = jnp.bfloat16
W = 256
H = 128
ROWS = 512
NB = 32

NN = (((1,), (0,)), ((), ()))
NT = (((1,), (1,)), ((), ()))
TN = (((0,), (0,)), ((), ()))


def remote(src, dst, send, recv, row, col):
    return pltpu.make_async_remote_copy(
        src_ref=src, dst_ref=dst, send_sem=send, recv_sem=recv,
        device_id={"row": row, "col": col}, device_id_type=MESH)


def split(x):
    hi = x.astype(BF16)
    return hi, (x - hi.astype(F32)).astype(BF16)


def dot(a, b, dims=NN, precision=None):
    return lax.dot_general(a, b, dims, precision=precision, preferred_element_type=F32)


def dot3(a, b, dims=NN):
    ah, al = split(a)
    bh, bl = split(b)
    return dot(ah, bh, dims) + (dot(ah, bl, dims) + dot(al, bh, dims))


def factorize(gram, work):
    lane = lax.broadcasted_iota(jnp.int32, (NB, 128), 1)
    sub = lax.broadcasted_iota(jnp.int32, (NB, 128), 0)
    eye = (lane == sub).astype(F32)
    for b in range(W // NB):
        lo = b * NB
        left = gram[lo:lo + NB, :]
        unit = (lax.broadcasted_iota(jnp.int32, (NB, W), 1) ==
                lax.broadcasted_iota(jnp.int32, (NB, W), 0) + lo).astype(F32)
        rows = jnp.concatenate([left, unit], axis=1)
        if b:
            rows = rows - dot(work[0:lo, lo:lo + NB], work[0:lo, :], TN, HIGHEST)
        tile = jnp.concatenate([rows[:, lo:lo + NB], eye[:, :NB], jnp.zeros((NB, 128 - 2 * NB), F32)], axis=1)
        for i in range(NB):
            row = tile[i:i + 1, :]
            factor = tile[:, i:i + 1] * (1.0 / tile[i:i + 1, i:i + 1])
            tile = jnp.where(sub > i, tile - factor * row, tile)
        pivots = jnp.sum(jnp.where(lane == sub, tile, 0.0), axis=1, keepdims=True)
        inverse = tile[:, NB:2 * NB] * lax.rsqrt(pivots)
        work[lo:lo + NB, :] = dot(inverse, rows, NN, HIGHEST)
        yield


def body(panel, a_hbm, factor_out, out_hbm,
         abuf, plh, yp, yq, rs, ytc, ptc, yz, yr, chi, clo, lhs,
         gpart, gpair, grs, gsum, spart, srs, szs, ssum, work,
         a_sem, o_sem, pair, rs_sem, ag_sem, sib_sem, z_sem, x_sem,
         px_send, px_recv, p0, py, psib, gp, gr, ga, gs, sr, sz, sa, ss):
    r = lax.axis_index("row")
    c = lax.axis_index("col")
    core = r % 2
    m = r // 2
    x = m % 4
    y = m // 4
    sib = r + 1 - 2 * core
    column = 2 * x + core
    source_x = c // 2
    source_core = c % 2
    on_source = x == source_x
    is_source = r % 8 == c
    is_second = jnp.logical_and(on_source, core != source_core)
    off_source = jnp.logical_not(on_source)
    mine = pl.ds(pl.multiple_of(core * H, H), H)
    other = pl.ds(pl.multiple_of(H - core * H, H), H)

    def in_plane(xx, yy, kk):
        return (yy * 4 + xx) * 2 + kk

    load = pltpu.make_async_copy(a_hbm, abuf, a_sem)
    load.start()

    barrier = pltpu.get_barrier_semaphore()

    def greet(row, col):
        pl.semaphore_signal(barrier, inc=1, device_id={"row": row, "col": col}, device_id_type=MESH)

    greet(sib, c)
    for d in range(1, 4):
        greet(in_plane((x + d) % 4, y, 1 - core), c)
    for p in range(1, 16):
        greet(((m + p) % 16) * 2 + core, c)
    for p in range(1, 8):
        greet(r, (c + p) % 8)

    flipped = panel[...].T
    high, low = split(flipped)
    plh[0:W, :] = high
    plh[W:, :] = low
    gpart[...] = dot(flipped, flipped, NT, HIGHEST)

    @pl.when(is_source)
    def _():
        for i in range(4):
            ptc[4 * y + i] = flipped[:, i * H:(i + 1) * H]

    pl.semaphore_wait(barrier, 26)

    def to_plane(src, dst, sems, p):
        return remote(src, dst, sems.at[0, p], sems.at[1, p], ((m + p) % 16) * 2 + core, c)

    def to_col(src, dst, sems, p):
        return remote(src, dst, sems.at[0, p], sems.at[1, p], r, (c + p) % 8)

    def to_sib(src, dst, sems, *at):
        return remote(src, dst, sems.at[(0, *at)], sems.at[(1, *at)], sib, c)

    def block(q):
        return pl.ds(4 * q, 4)

    gram_pair = to_sib(gpart.at[other, :], gpair, gp)
    gram_pair.start()

    own_half = ptc.at[block(y), mine, :]
    whole = ptc.at[block(y), :, :]

    def px_copy(d, k):
        ref = ptc.at[block(y), k * H:(k + 1) * H, :]
        return remote(ref, ref, px_send.at[d - 1, k], px_recv, in_plane((x + d) % 4, y, k), c)

    share_whole = to_sib(whole, whole, p0)
    share_half = to_sib(own_half, own_half, p0)

    @pl.when(is_source)
    def _():
        share_whole.start()
        for d in (2, 1, 3):
            for k in range(2):
                px_copy(d, k).start()

    def small_out(part, slots, sems):
        for p in range(1, 16):
            rows = pl.ds(pl.multiple_of(((m + p) % 16) * 8, 8), 8)
            yield to_plane(part.at[rows, :], slots.at[p], sems, p)

    def small_back(total, sems, arriving):
        for p in range(1, 16):
            at = (m + 16 - p) % 16 if arriving else m
            ref = total.at[pl.ds(pl.multiple_of(core * H + at * 8, 8), 8), :]
            yield to_plane(ref, ref, sems, p)

    def small_sum(part, slots):
        value = part[pl.ds(pl.multiple_of(m * 8, 8), 8), :]
        for p in range(1, 16):
            value = value + slots[p]
        return value

    own_rows = pl.ds(pl.multiple_of(core * H + m * 8, 8), 8)

    gram_pair.wait_recv()
    gpair[...] = gpair[...] + gpart[mine, :]
    for copy in small_out(gpair, grs, gr):
        copy.start()

    load.wait()
    for q in range(4):
        value = jnp.concatenate([abuf[pl.ds(4 * i + q, ROWS, stride=16), :] for i in range(4)], axis=1)
        ah, al = split(value)
        both = dot(plh[...], ah)
        value = both[0:W] + (both[W:] + dot(plh[0:W, :], al))
        for i in range(4):
            yp[4 * q + i] = value[:, i * H:(i + 1) * H]
        to_sib(yp.at[4 * q:4 * q + 4, other, :], yq.at[4 * q:4 * q + 4], pair, q).start()

    for copy in small_out(gpair, grs, gr):
        copy.wait_recv()
    gsum[own_rows, :] = small_sum(gpair, grs)
    for copy in small_back(gsum, ga, False):
        copy.start()

    def pair_copy(q):
        return to_sib(yp.at[4 * q:4 * q + 4, other, :], yq.at[4 * q:4 * q + 4], pair, q)

    for q in range(4):
        pair_copy(q).wait_recv()
        for i in range(4):
            yp[4 * q + i, mine, :] = yp[4 * q + i, mine, :] + yq[4 * q + i]

    def rs_copy(p):
        return to_plane(yp.at[(m + p) % 16, mine, :], rs.at[p], rs_sem, p)

    for p in range(1, 16):
        rs_copy(p).start()

    for copy in small_back(gsum, ga, True):
        copy.wait_recv()
    gram_share = to_sib(gsum.at[mine, :], gsum.at[mine, :], gs)
    gram_share.start()
    to_sib(gsum.at[other, :], gsum.at[other, :], gs).wait_recv()

    blocks = factorize(gsum, work)
    next(blocks)

    @pl.when(is_second)
    def _():
        share_whole.wait_recv()

    @pl.when(off_source)
    def _():
        remote(own_half, own_half, px_send.at[0, 0], px_recv, sib, c).wait_recv()
        share_half.start()

    next(blocks)

    @pl.when(off_source)
    def _():
        theirs = ptc.at[block(y), other, :]
        to_sib(theirs, theirs, p0).wait_recv()

    next(blocks)

    for p in range(1, 16):
        rs_copy(p).wait_recv()
    piece = yp[m, mine, :]
    for p in range(1, 16):
        piece = piece + rs[p]
    ytc[m, mine, :] = piece
    own = ytc.at[m, mine, :]

    spart[...] = dot3(piece, ptc[m], NT)
    for copy in small_out(spart, srs, sr):
        copy.start()

    def z_copy(p):
        return to_col(own, yz.at[p], z_sem, p)

    def ag_copy(p, arriving):
        at = (m + 16 - p) % 16 if arriving else m
        ref = ytc.at[at, mine, :]
        return to_plane(ref, ref, ag_sem, p)

    def py_copy(d, arriving):
        at = (y + 4 - d) % 4 if arriving else y
        ref = ptc.at[block(at), mine, :]
        return remote(ref, ref, py.at[0, d - 1], py.at[1, d - 1], in_plane(x, (y + d) % 4, core), c)

    for p in range(1, 8):
        z_copy(p).start()
    for p in range(1, 16):
        ag_copy(p, False).start()
    for d in range(1, 4):
        py_copy(d, False).start()

    def x_copy(p):
        place = (c + 8 - p) % 8
        src = own if p == 0 else yz.at[p]
        return remote(src, yr.at[x, mine, :], x_sem.at[0, p], x_sem.at[1, column],
                      in_plane(place // 2, y, place % 2), c)

    def x_start(p):
        at_home = (c + 8 - p) % 8 == column

        @pl.when(at_home)
        def _():
            yr[x, mine, :] = ytc[m, mine, :] if p == 0 else yz[p]

        @pl.when(jnp.logical_not(at_home))
        def _():
            x_copy(p).start()

    x_start(0)
    next(blocks)
    for copy in small_out(spart, srs, sr):
        copy.wait_recv()
    szs[0] = small_sum(spart, srs)
    for p in range(1, 8):
        to_col(szs.at[0], szs.at[p], sz, p).start()
    next(blocks)
    for p in range(1, 8):
        to_col(szs.at[0], szs.at[p], sz, p).wait_recv()
    value = szs[0]
    for p in range(1, 8):
        value = value + szs[p]
    ssum[own_rows, :] = value
    for copy in small_back(ssum, sa, False):
        copy.start()
    next(blocks)
    for p in range(1, 8):
        z_copy(p).wait_recv()
        x_start(p)
    next(blocks)
    for copy in small_back(ssum, sa, True):
        copy.wait_recv()
    cross_share = to_sib(ssum.at[mine, :], ssum.at[mine, :], ss)
    cross_share.start()
    next(blocks)

    upper = lax.broadcasted_iota(jnp.int32, (W, W), 1) >= lax.broadcasted_iota(jnp.int32, (W, W), 0)
    factor_out[...] = jnp.where(upper, work[:, :W], 0.0)
    inverse = work[:, W:]
    metric = dot(inverse, inverse, TN, HIGHEST)
    first = 2.0 * dot3(panel[...], metric)
    lhs[0:ROWS, :W], lhs[ROWS:, :W] = split(first)

    def piece_share(p, arriving):
        at = (m + 16 - p) % 16
        ref = ytc.at[at, other if arriving else mine, :]
        return to_sib(ref, ref, sib_sem, p)

    def block_share(d, arriving):
        ref = ptc.at[block((y + 4 - d) % 4), other if arriving else mine, :]
        return to_sib(ref, ref, psib, d - 1)

    piece_share(0, False).start()
    for p in range(1, 16):
        ag_copy(p, True).wait_recv()
        piece_share(p, False).start()
    for d in range(1, 4):
        py_copy(d, True).wait_recv()
        block_share(d, False).start()

    to_sib(ssum.at[other, :], ssum.at[other, :], ss).wait_recv()
    for u in range(8):
        @pl.when(column != u)
        def _():
            ref = yr.at[u // 2, (u % 2) * H:(u % 2 + 1) * H, :]
            remote(ref, ref, x_sem.at[0, 0], x_sem.at[1, u], sib, c).wait_recv()
    image = jnp.concatenate([yr[i].T for i in range(4)], axis=0)
    second = 2.0 * dot3(image - dot3(first, ssum[...]), metric)
    lhs[0:ROWS, W:], lhs[ROWS:, W:] = split(second)

    for p in range(16):
        piece_share(p, True).wait_recv()
    for d in range(1, 4):
        block_share(d, True).wait_recv()

    for q in range(4):
        for i in range(4):
            lanes = pl.ds(i * H, H)
            chi[q, 0:W, lanes], clo[q, 0:W, lanes] = split(ytc[4 * q + i])
            chi[q, W:, lanes], clo[q, W:, lanes] = split(ptc[4 * q + i])
    half = ROWS // 2
    for s in range(2):
        lh = lhs[s * half:(s + 1) * half, :]
        ll = lhs[ROWS + s * half:ROWS + (s + 1) * half, :]
        for q in range(4):
            value = dot(lh, chi[q]) + (dot(ll, chi[q]) + dot(lh, clo[q]))
            for i in range(4):
                at = pl.ds(s * half * 16 + 4 * i + q, half, stride=16)
                abuf[at, :] = abuf[at, :] - value[:, i * H:(i + 1) * H]
        rows = pl.ds(s * half * 16, half * 16)
        pltpu.make_async_copy(abuf.at[rows, :], out_hbm.at[rows, :], o_sem.at[s]).start()

    gram_pair.wait_send()
    gram_share.wait_send()
    cross_share.wait_send()

    @pl.when(is_source)
    def _():
        share_whole.wait_send()
        for d in range(1, 4):
            for k in range(2):
                px_copy(d, k).wait_send()

    @pl.when(off_source)
    def _():
        share_half.wait_send()

    for q in range(4):
        pair_copy(q).wait_send()
    for d in range(1, 4):
        py_copy(d, False).wait_send()
        block_share(d, False).wait_send()
    for p in range(16):
        piece_share(p, False).wait_send()
        if p:
            rs_copy(p).wait_send()
            ag_copy(p, False).wait_send()
    for copies in (small_out(gpair, grs, gr), small_back(gsum, ga, False),
                   small_out(spart, srs, sr), small_back(ssum, sa, False)):
        for copy in copies:
            copy.wait_send()
    for p in range(8):
        @pl.when((c + 8 - p) % 8 != column)
        def _():
            x_copy(p).wait_send()

        if p:
            z_copy(p).wait_send()
            to_col(szs.at[0], szs.at[p], sz, p).wait_send()
    for s in range(2):
        rows = pl.ds(s * half * 16, half * 16)
        pltpu.make_async_copy(abuf.at[rows, :], out_hbm.at[rows, :], o_sem.at[s]).wait()


def shards(panel, matrix):
    vmem = pltpu.VMEM
    dma = pltpu.SemaphoreType.DMA
    factor, updated = pl.pallas_call(
        body,
        out_shape=(jax.ShapeDtypeStruct((W, W), F32), jax.ShapeDtypeStruct((ROWS * 16, H), F32)),
        in_specs=[pl.BlockSpec(memory_space=pltpu.VMEM), pl.BlockSpec(memory_space=pl.ANY)],
        out_specs=(pl.BlockSpec(memory_space=pltpu.VMEM), pl.BlockSpec(memory_space=pl.ANY)),
        scratch_shapes=[
            vmem((ROWS * 16, H), F32), vmem((2 * W, ROWS), BF16),
            vmem((16, W, H), F32), vmem((16, H, H), F32), vmem((16, H, H), F32),
            vmem((16, W, H), F32), vmem((16, W, H), F32), vmem((8, H, H), F32), vmem((4, W, H), F32),
            vmem((4, 2 * W, ROWS), BF16), vmem((4, 2 * W, ROWS), BF16), vmem((2 * ROWS, 2 * W), BF16),
            vmem((W, W), F32), vmem((H, W), F32), vmem((16, 8, W), F32), vmem((W, W), F32),
            vmem((H, W), F32), vmem((16, 8, W), F32), vmem((8, 8, W), F32), vmem((W, W), F32),
            vmem((W, 2 * W), F32),
            dma, dma((2,)), dma((2, 4)), dma((2, 16)), dma((2, 16)), dma((2, 16)), dma((2, 8)), dma((2, 8)),
            dma((3, 2)), dma, dma((2,)), dma((2, 3)), dma((2, 3)),
            dma((2,)), dma((2, 16)), dma((2, 16)), dma((2,)),
            dma((2, 16)), dma((2, 8)), dma((2, 16)), dma((2,)),
        ],
        compiler_params=pltpu.CompilerParams(
            collective_id=0, has_side_effects=True, vmem_limit_bytes=56 * 2**20),
        cost_estimate=pl.CostEstimate(flops=5 * 10**9, bytes_accessed=9 * 2**20, transcendentals=0),
    )(panel.reshape(ROWS, W), matrix.reshape(ROWS * 16, H))
    return factor, updated.reshape(matrix.shape)


def solution(mesh):
    in_specs = (P(None, "row", None), P(None, "row", None, "col"))
    out_specs = (P(), P(None, "row", None, "col"))
    return jax.shard_map(shards, mesh=mesh, in_specs=in_specs, out_specs=out_specs, check_vma=False)
```

```python
import jax
import jax.numpy as jnp
from jax import lax
from jax.experimental import pallas as pl
from jax.experimental.pallas import tpu as pltpu
from jax.sharding import PartitionSpec as P

MESH = pl.DeviceIdType.MESH
HIGHEST = lax.Precision.HIGHEST
F32 = jnp.float32
BF16 = jnp.bfloat16
W = 256
H = 128
ROWS = 512
NB = 32

NN = (((1,), (0,)), ((), ()))
NT = (((1,), (1,)), ((), ()))
TN = (((0,), (0,)), ((), ()))


def remote(src, dst, send, recv, row, col):
    return pltpu.make_async_remote_copy(
        src_ref=src, dst_ref=dst, send_sem=send, recv_sem=recv,
        device_id={"row": row, "col": col}, device_id_type=MESH)


def split(x):
    hi = x.astype(BF16)
    return hi, (x - hi.astype(F32)).astype(BF16)


def dot(a, b, dims=NN, precision=None):
    return lax.dot_general(a, b, dims, precision=precision, preferred_element_type=F32)


def dot3(a, b, dims=NN):
    ah, al = split(a)
    bh, bl = split(b)
    return dot(ah, bh, dims) + (dot(ah, bl, dims) + dot(al, bh, dims))


def eliminate(tile):
    sub = lax.broadcasted_iota(jnp.int32, (8, 128), 0)
    groups = NB // 8
    rows = [tile[8 * g:8 * g + 8] for g in range(groups)]
    for g in range(groups):
        cols = [[jnp.broadcast_to(rows[h][:, 8 * g + k:8 * g + k + 1], (8, 128)) for h in range(g, groups)]
                for k in range(8)]
        for j in range(8):
            inverse = 1.0 / cols[j][0][j:j + 1]
            scaled = rows[g][j:j + 1] * inverse
            for k in range(j + 1, 8):
                ratio = cols[k][0][j:j + 1] * inverse
                cols[k] = [a - b * ratio for a, b in zip(cols[k], cols[j])]
            rows[g] = jnp.where(sub > j, rows[g] - cols[j][0] * scaled, rows[g])
            for h in range(g + 1, groups):
                rows[h] = rows[h] - cols[j][h - g] * scaled
    return jnp.concatenate(rows, axis=0)


def factorize(gram, work):
    lane = lax.broadcasted_iota(jnp.int32, (NB, 128), 1)
    sub = lax.broadcasted_iota(jnp.int32, (NB, 128), 0)
    eye = (lane == sub).astype(F32)
    work[...] = jnp.zeros_like(work)
    for b in range(W // NB):
        lo = b * NB
        start = lo // 128 * 128
        span = (lo + NB + 127) // 128 * 128
        unit = (lax.broadcasted_iota(jnp.int32, (NB, span), 1) ==
                lax.broadcasted_iota(jnp.int32, (NB, span), 0) + lo).astype(F32)
        rows = jnp.concatenate([gram[lo:lo + NB, start:], unit], axis=1)
        if b:
            rows = rows - dot(work[0:lo, lo:lo + NB], work[0:lo, start:W + span], TN, HIGHEST)
        square = rows[:, lo - start:lo - start + NB]
        tile = eliminate(jnp.concatenate([square, eye[:, :NB], jnp.zeros((NB, 128 - 2 * NB), F32)], axis=1))
        pivots = jnp.sum(jnp.where(lane == sub, tile, 0.0), axis=1, keepdims=True)
        inverse = tile[:, NB:2 * NB] * lax.rsqrt(pivots)
        work[lo:lo + NB, start:W + span] = dot(inverse, rows, NN, HIGHEST)
        yield


def body(panel, a_hbm, factor_out, updated,
         abuf, plh, yp, yq, rs, ytc, ptc, yz, yr, chi, clo, lhs,
         gpart, gpair, gps, gsum, spart, szs, sps, ssum, work,
         a_sem, pair, rs_sem, ag_sem, sib_sem, z_sem, x_sem,
         px_send, px_recv, p0, py, psib, gp, gr, ga, gs, sz, sr, sa, ss):
    r = lax.axis_index("row")
    c = lax.axis_index("col")
    core = r % 2
    m = r // 2
    x = m % 4
    y = m // 4
    sib = r + 1 - 2 * core
    column = 2 * x + core
    source_x = c // 2
    source_core = c % 2
    on_source = x == source_x
    is_source = r % 8 == c
    is_second = jnp.logical_and(on_source, core != source_core)
    off_source = jnp.logical_not(on_source)
    mine = pl.ds(pl.multiple_of(core * H, H), H)
    other = pl.ds(pl.multiple_of(H - core * H, H), H)

    def in_plane(xx, yy, kk):
        return (yy * 4 + xx) * 2 + kk

    load = pltpu.make_async_copy(a_hbm, abuf, a_sem)
    load.start()

    barrier = pltpu.get_barrier_semaphore()

    def greet(row, col):
        pl.semaphore_signal(barrier, inc=1, device_id={"row": row, "col": col}, device_id_type=MESH)

    greet(sib, c)
    for d in range(1, 4):
        greet(in_plane((x + d) % 4, y, 1 - core), c)
    for p in range(1, 16):
        greet(((m + p) % 16) * 2 + core, c)
    for p in range(1, 8):
        greet(r, (c + p) % 8)

    flipped = panel[...].T
    high, low = split(flipped)
    plh[0:W, :] = high
    plh[W:, :] = low
    gpart[...] = dot(flipped, flipped, NT, HIGHEST)

    @pl.when(is_source)
    def _():
        for i in range(4):
            ptc[4 * y + i] = flipped[:, i * H:(i + 1) * H]

    pl.semaphore_wait(barrier, 26)

    def to_plane(src, dst, sems, p):
        return remote(src, dst, sems.at[0, p], sems.at[1, p], ((m + p) % 16) * 2 + core, c)

    def to_col(src, dst, sems, p):
        return remote(src, dst, sems.at[0, p], sems.at[1, p], r, (c + p) % 8)

    def to_sib(src, dst, sems, *at):
        return remote(src, dst, sems.at[(0, *at)], sems.at[(1, *at)], sib, c)

    def block(q):
        return pl.ds(4 * q, 4)

    gram_pair = to_sib(gpart.at[pl.ds(pl.multiple_of(H - core * H + c * 16, 16), 16), :], gpair, gp)
    gram_pair.start()

    own_half = ptc.at[block(y), mine, :]
    whole = ptc.at[block(y), :, :]

    def px_copy(d, k):
        ref = ptc.at[block(y), k * H:(k + 1) * H, :]
        return remote(ref, ref, px_send.at[d - 1, k], px_recv, in_plane((x + d) % 4, y, k), c)

    share_whole = to_sib(whole, whole, p0)
    share_half = to_sib(own_half, own_half, p0)

    @pl.when(is_source)
    def _():
        share_whole.start()
        for d in (2, 1, 3):
            for k in range(2):
                px_copy(d, k).start()

    own_rows = pl.ds(pl.multiple_of(core * H + c * 16, 16), 16)

    def spread_plane(slots, sems):
        for p in range(1, 16):
            yield to_plane(slots.at[0], slots.at[p], sems, p)

    def spread_col(total, sems, arriving):
        for p in range(1, 8):
            at = (c + 8 - p) % 8 if arriving else c
            ref = total.at[pl.ds(pl.multiple_of(core * H + at * 16, 16), 16), :]
            yield to_col(ref, ref, sems, p)

    def sum_slots(slots, n):
        value = slots[0]
        for p in range(1, n):
            value = value + slots[p]
        return value

    gram_pair.wait_recv()
    gps[0] = gpair[...] + gpart[own_rows, :]
    for copy in spread_plane(gps, gr):
        copy.start()

    def pair_copy(s):
        return to_sib(yp.at[block((y + s) % 4), other, :], yq.at[4 * s:4 * s + 4], pair, s)

    def rs_copy(s, i):
        target = 4 * ((y + s) % 4) + i
        return remote(yp.at[target, mine, :], rs.at[m], rs_sem.at[0, 4 * s + i], rs_sem.at[1, m], target * 2 + core, c)

    def scatter(s):
        pair_copy(s).wait_recv()
        for i in range(4):
            at = 4 * ((y + s) % 4) + i
            yp[at, mine, :] = yp[at, mine, :] + yq[4 * s + i]
            if s:
                rs_copy(s, i).start()
            else:
                @pl.when(x != i)
                def _():
                    rs_copy(s, i).start()

                @pl.when(x == i)
                def _():
                    rs[m] = yp[m, mine, :]

    load.wait()
    order = (2, 1, 3, 0)
    for n, s in enumerate(order):
        q = (y + s) % 4
        value = jnp.concatenate([abuf[pl.ds(4 * i + q, ROWS, stride=16), :] for i in range(4)], axis=1)
        ah, al = split(value)
        both = dot(plh[...], ah)
        value = both[0:W] + (both[W:] + dot(plh[0:W, :], al))
        for i in range(4):
            yp[4 * q + i] = value[:, i * H:(i + 1) * H]
        pair_copy(s).start()
        if n:
            scatter(order[n - 1])
    scatter(order[-1])

    for copy in spread_plane(gps, gr):
        copy.wait_recv()
    gsum[own_rows, :] = sum_slots(gps, 16)
    for copy in spread_col(gsum, ga, False):
        copy.start()

    @pl.when(is_second)
    def _():
        share_whole.wait_recv()

    @pl.when(off_source)
    def _():
        remote(own_half, own_half, px_send.at[0, 0], px_recv, sib, c).wait_recv()
        share_half.start()

    for copy in spread_col(gsum, ga, True):
        copy.wait_recv()
    gram_share = to_sib(gsum.at[mine, :], gsum.at[mine, :], gs)
    gram_share.start()
    to_sib(gsum.at[other, :], gsum.at[other, :], gs).wait_recv()

    for u in range(16):
        @pl.when(m != u)
        def _():
            remote(rs.at[u], rs.at[u], rs_sem.at[0, 0], rs_sem.at[1, u], sib, c).wait_recv()
    piece = sum_slots(rs, 16)
    ytc[m, mine, :] = piece
    own = ytc.at[m, mine, :]

    @pl.when(off_source)
    def _():
        theirs = ptc.at[block(y), other, :]
        to_sib(theirs, theirs, p0).wait_recv()

    def cross_copy(p):
        rows = pl.ds(pl.multiple_of((c + p) % 8 * 16, 16), 16)
        return to_col(spart.at[rows, :], szs.at[p], sz, p)

    spart[...] = dot3(piece, ptc[m], NT)
    for p in range(1, 8):
        cross_copy(p).start()

    def z_copy(p):
        return to_col(own, yz.at[p], z_sem, p)

    def ag_copy(p, arriving):
        at = (m + 16 - p) % 16 if arriving else m
        ref = ytc.at[at, mine, :]
        return to_plane(ref, ref, ag_sem, p)

    def py_copy(d, arriving):
        at = (y + 4 - d) % 4 if arriving else y
        ref = ptc.at[block(at), mine, :]
        return remote(ref, ref, py.at[0, d - 1], py.at[1, d - 1], in_plane(x, (y + d) % 4, core), c)

    for p in range(1, 8):
        z_copy(p).start()
    for p in range(1, 16):
        ag_copy(p, False).start()

    def x_copy(p):
        place = (c + 8 - p) % 8
        src = own if p == 0 else yz.at[p]
        return remote(src, yr.at[x, mine, :], x_sem.at[0, p], x_sem.at[1, column],
                      in_plane(place // 2, y, place % 2), c)

    def x_start(p):
        at_home = (c + 8 - p) % 8 == column

        @pl.when(at_home)
        def _():
            yr[x, mine, :] = ytc[m, mine, :] if p == 0 else yz[p]

        @pl.when(jnp.logical_not(at_home))
        def _():
            x_copy(p).start()

    x_start(0)
    blocks = factorize(gsum, work)
    for _ in range(4):
        next(blocks)
    szs[0] = spart[pl.ds(pl.multiple_of(c * 16, 16), 16), :]
    for p in range(1, 8):
        cross_copy(p).wait_recv()
    sps[0] = sum_slots(szs, 8)
    for copy in spread_plane(sps, sr):
        copy.start()
    for d in range(1, 4):
        py_copy(d, False).start()
    for _ in range(4):
        next(blocks)
    for p in range(1, 8):
        z_copy(p).wait_recv()
        x_start(p)
    for copy in spread_plane(sps, sr):
        copy.wait_recv()
    ssum[own_rows, :] = sum_slots(sps, 16)
    for copy in spread_col(ssum, sa, False):
        copy.start()

    upper = lax.broadcasted_iota(jnp.int32, (W, W), 1) >= lax.broadcasted_iota(jnp.int32, (W, W), 0)
    factor_out[...] = jnp.where(upper, work[:, :W], 0.0)
    inverse = work[:, W:]
    metric = dot(inverse, inverse, TN, HIGHEST)
    first = 2.0 * dot3(panel[...], metric)
    lhs[0:ROWS, :W], lhs[ROWS:, :W] = split(first)

    def piece_share(p, arriving):
        at = (m + 16 - p) % 16
        ref = ytc.at[at, other if arriving else mine, :]
        return to_sib(ref, ref, sib_sem, p)

    def block_share(d, arriving):
        ref = ptc.at[block((y + 4 - d) % 4), other if arriving else mine, :]
        return to_sib(ref, ref, psib, d - 1)

    piece_share(0, False).start()
    for p in range(1, 16):
        ag_copy(p, True).wait_recv()
        piece_share(p, False).start()
    for copy in spread_col(ssum, sa, True):
        copy.wait_recv()
    cross_share = to_sib(ssum.at[mine, :], ssum.at[mine, :], ss)
    cross_share.start()
    for d in range(1, 4):
        py_copy(d, True).wait_recv()
        block_share(d, False).start()

    to_sib(ssum.at[other, :], ssum.at[other, :], ss).wait_recv()
    for u in range(8):
        @pl.when(column != u)
        def _():
            ref = yr.at[u // 2, (u % 2) * H:(u % 2 + 1) * H, :]
            remote(ref, ref, x_sem.at[0, 0], x_sem.at[1, u], sib, c).wait_recv()
    image = jnp.concatenate([yr[i].T for i in range(4)], axis=0)
    second = 2.0 * dot3(image - dot3(first, ssum[...]), metric)
    lhs[0:ROWS, W:], lhs[ROWS:, W:] = split(second)

    for p in range(16):
        piece_share(p, True).wait_recv()
    for d in range(1, 4):
        block_share(d, True).wait_recv()

    for q in range(4):
        for i in range(4):
            lanes = pl.ds(i * H, H)
            chi[q, 0:W, lanes], clo[q, 0:W, lanes] = split(ytc[4 * q + i])
            chi[q, W:, lanes], clo[q, W:, lanes] = split(ptc[4 * q + i])
    half = ROWS // 2
    for s in range(2):
        lh = lhs[s * half:(s + 1) * half, :]
        ll = lhs[ROWS + s * half:ROWS + (s + 1) * half, :]
        for q in range(4):
            value = dot(lh, chi[q]) + (dot(ll, chi[q]) + dot(lh, clo[q]))
            for i in range(4):
                at = pl.ds(s * half * 16 + 4 * i + q, half, stride=16)
                updated[at, :] = abuf[at, :] - value[:, i * H:(i + 1) * H]

    gram_pair.wait_send()
    gram_share.wait_send()
    cross_share.wait_send()

    @pl.when(is_source)
    def _():
        share_whole.wait_send()
        for d in range(1, 4):
            for k in range(2):
                px_copy(d, k).wait_send()

    @pl.when(off_source)
    def _():
        share_half.wait_send()

    for s in range(4):
        pair_copy(s).wait_send()
        for i in range(4):
            if s:
                rs_copy(s, i).wait_send()
            else:
                @pl.when(x != i)
                def _():
                    rs_copy(s, i).wait_send()

    for d in range(1, 4):
        py_copy(d, False).wait_send()
        block_share(d, False).wait_send()
    for p in range(16):
        piece_share(p, False).wait_send()
        if p:
            ag_copy(p, False).wait_send()
    for copies in (spread_plane(gps, gr), spread_col(gsum, ga, False),
                   spread_plane(sps, sr), spread_col(ssum, sa, False)):
        for copy in copies:
            copy.wait_send()
    for p in range(8):
        @pl.when((c + 8 - p) % 8 != column)
        def _():
            x_copy(p).wait_send()

        if p:
            z_copy(p).wait_send()
            cross_copy(p).wait_send()


def shards(panel, matrix):
    vmem = pltpu.VMEM
    dma = pltpu.SemaphoreType.DMA
    factor, result = pl.pallas_call(
        body,
        out_shape=(pltpu.VMEM((W, W), F32), pltpu.VMEM((ROWS * 16, H), F32)),
        in_specs=[pl.BlockSpec(memory_space=pltpu.VMEM), pl.BlockSpec(memory_space=pltpu.HBM)],
        out_specs=(pl.BlockSpec(memory_space=pltpu.VMEM), pl.BlockSpec(memory_space=pltpu.VMEM)),
        scratch_shapes=[
            vmem((ROWS * 16, H), F32), vmem((2 * W, ROWS), BF16),
            vmem((16, W, H), F32), vmem((16, H, H), F32), vmem((16, H, H), F32),
            vmem((16, W, H), F32), vmem((16, W, H), F32), vmem((8, H, H), F32), vmem((4, W, H), F32),
            vmem((4, 2 * W, ROWS), BF16), vmem((4, 2 * W, ROWS), BF16), vmem((2 * ROWS, 2 * W), BF16),
            vmem((W, W), F32), vmem((16, W), F32), vmem((16, 16, W), F32), vmem((W, W), F32),
            vmem((H, W), F32), vmem((8, 16, W), F32), vmem((16, 16, W), F32), vmem((W, W), F32),
            vmem((W, 2 * W), F32),
            dma, dma((2, 4)), dma((2, 16)), dma((2, 16)), dma((2, 16)), dma((2, 8)), dma((2, 8)),
            dma((3, 2)), dma, dma((2,)), dma((2, 3)), dma((2, 3)),
            dma((2,)), dma((2, 16)), dma((2, 8)), dma((2,)),
            dma((2, 8)), dma((2, 16)), dma((2, 8)), dma((2,)),
        ],
        compiler_params=pltpu.CompilerParams(
            collective_id=0, has_side_effects=True, vmem_limit_bytes=54 * 2**20),
        cost_estimate=pl.CostEstimate(flops=5 * 10**9, bytes_accessed=9 * 2**20, transcendentals=0),
    )(panel.reshape(ROWS, W), matrix.reshape(ROWS * 16, H))
    return factor, result.reshape(matrix.shape)


def solution(mesh):
    in_specs = (P(None, "row", None), P(None, "row", None, "col"))
    out_specs = (P(), P(None, "row", None, "col"))
    return jax.shard_map(shards, mesh=mesh, in_specs=in_specs, out_specs=out_specs, check_vma=False)
```

```python
import jax
import jax.numpy as jnp
from jax import lax
from jax.experimental import pallas as pl
from jax.experimental.pallas import tpu as pltpu
from jax.sharding import PartitionSpec as P

MESH = pl.DeviceIdType.MESH
HIGHEST = lax.Precision.HIGHEST
F32 = jnp.float32
BF16 = jnp.bfloat16
W = 256
H = 128
ROWS = 512
NB = 32

NN = (((1,), (0,)), ((), ()))
NT = (((1,), (1,)), ((), ()))
TN = (((0,), (0,)), ((), ()))


def remote(src, dst, send, recv, row, col):
    return pltpu.make_async_remote_copy(
        src_ref=src, dst_ref=dst, send_sem=send, recv_sem=recv,
        device_id={"row": row, "col": col}, device_id_type=MESH)


def split(x):
    hi = x.astype(BF16)
    return hi, (x - hi.astype(F32)).astype(BF16)


def dot(a, b, dims=NN, precision=None):
    return lax.dot_general(a, b, dims, precision=precision, preferred_element_type=F32)


def dot3(a, b, dims=NN):
    ah, al = split(a)
    bh, bl = split(b)
    return dot(ah, bh, dims) + (dot(ah, bl, dims) + dot(al, bh, dims))


def eliminate(tile):
    sub = lax.broadcasted_iota(jnp.int32, (8, 128), 0)
    groups = NB // 8
    rows = [tile[8 * g:8 * g + 8] for g in range(groups)]
    for g in range(groups):
        cols = [[jnp.broadcast_to(rows[h][:, 8 * g + k:8 * g + k + 1], (8, 128)) for h in range(g, groups)]
                for k in range(8)]
        for j in range(8):
            inverse = 1.0 / cols[j][0][j:j + 1]
            scaled = rows[g][j:j + 1] * inverse
            for k in range(j + 1, 8):
                ratio = cols[k][0][j:j + 1] * inverse
                cols[k] = [a - b * ratio for a, b in zip(cols[k], cols[j])]
            rows[g] = jnp.where(sub > j, rows[g] - cols[j][0] * scaled, rows[g])
            for h in range(g + 1, groups):
                rows[h] = rows[h] - cols[j][h - g] * scaled
    return jnp.concatenate(rows, axis=0)


def factorize(gram, work):
    lane = lax.broadcasted_iota(jnp.int32, (NB, 128), 1)
    sub = lax.broadcasted_iota(jnp.int32, (NB, 128), 0)
    eye = (lane == sub).astype(F32)
    work[...] = jnp.zeros_like(work)
    for b in range(W // NB):
        lo = b * NB
        start = lo // 128 * 128
        span = (lo + NB + 127) // 128 * 128
        unit = (lax.broadcasted_iota(jnp.int32, (NB, span), 1) ==
                lax.broadcasted_iota(jnp.int32, (NB, span), 0) + lo).astype(F32)
        rows = jnp.concatenate([gram[lo:lo + NB, start:], unit], axis=1)
        if b:
            rows = rows - dot(work[0:lo, lo:lo + NB], work[0:lo, start:W + span], TN, HIGHEST)
        square = rows[:, lo - start:lo - start + NB]
        tile = eliminate(jnp.concatenate([square, eye[:, :NB], jnp.zeros((NB, 128 - 2 * NB), F32)], axis=1))
        pivots = jnp.sum(jnp.where(lane == sub, tile, 0.0), axis=1, keepdims=True)
        inverse = tile[:, NB:2 * NB] * lax.rsqrt(pivots)
        work[lo:lo + NB, start:W + span] = dot(inverse, rows, NN, HIGHEST)
        yield


def body(panel, a_hbm, factor_out, updated,
         abuf, plh, yp, yq, rs, ytc, ptc, yz, yr, chi, clo, lhs,
         gpart, gpair, gps, gsum, spart, szs, sps, ssum, work,
         a_sem, pair, rs_sem, ag_sem, sib_sem, z_sem, x_sem,
         px_send, px_recv, p0, py, psib, gp, gr, ga, gs, sz, sr, sa, ss):
    r = lax.axis_index("row")
    c = lax.axis_index("col")
    core = r % 2
    m = r // 2
    x = m % 4
    y = m // 4
    sib = r + 1 - 2 * core
    column = 2 * x + core
    source_x = c // 2
    source_core = c % 2
    on_source = x == source_x
    is_source = r % 8 == c
    is_second = jnp.logical_and(on_source, core != source_core)
    off_source = jnp.logical_not(on_source)
    mine = pl.ds(pl.multiple_of(core * H, H), H)
    other = pl.ds(pl.multiple_of(H - core * H, H), H)

    def in_plane(xx, yy, kk):
        return (yy * 4 + xx) * 2 + kk

    load = pltpu.make_async_copy(a_hbm, abuf, a_sem)
    load.start()

    barrier = pltpu.get_barrier_semaphore()

    def greet(row, col):
        pl.semaphore_signal(barrier, inc=1, device_id={"row": row, "col": col}, device_id_type=MESH)

    greet(sib, c)
    for d in range(1, 4):
        greet(in_plane((x + d) % 4, y, 1 - core), c)
    for p in range(1, 16):
        greet(((m + p) % 16) * 2 + core, c)
    for p in range(1, 8):
        greet(r, (c + p) % 8)

    flipped = panel[...].T
    high, low = split(flipped)
    plh[0:W, :] = high
    plh[W:, :] = low
    gpart[...] = dot(flipped, flipped, NT, HIGHEST)

    @pl.when(is_source)
    def _():
        for i in range(4):
            ptc[4 * y + i] = flipped[:, i * H:(i + 1) * H]

    pl.semaphore_wait(barrier, 26)

    def to_plane(src, dst, sems, p):
        return remote(src, dst, sems.at[0, p], sems.at[1, p], ((m + p) % 16) * 2 + core, c)

    def to_col(src, dst, sems, p):
        return remote(src, dst, sems.at[0, p], sems.at[1, p], r, (c + p) % 8)

    def to_sib(src, dst, sems, *at):
        return remote(src, dst, sems.at[(0, *at)], sems.at[(1, *at)], sib, c)

    def block(q):
        return pl.ds(4 * q, 4)

    gram_pair = to_sib(gpart.at[pl.ds(pl.multiple_of(H - core * H + c * 16, 16), 16), :], gpair, gp)
    gram_pair.start()

    own_half = ptc.at[block(y), mine, :]
    whole = ptc.at[block(y), :, :]

    def px_copy(d, k):
        ref = ptc.at[block(y), k * H:(k + 1) * H, :]
        return remote(ref, ref, px_send.at[d - 1, k], px_recv, in_plane((x + d) % 4, y, k), c)

    share_whole = to_sib(whole, whole, p0)
    share_half = to_sib(own_half, own_half, p0)

    @pl.when(is_source)
    def _():
        share_whole.start()
        for d in (2, 1, 3):
            for k in range(2):
                px_copy(d, k).start()

    own_rows = pl.ds(pl.multiple_of(core * H + c * 16, 16), 16)

    def spread_plane(slots, sems):
        for p in range(1, 16):
            yield to_plane(slots.at[0], slots.at[p], sems, p)

    def spread_col(total, sems, arriving):
        for p in range(1, 8):
            at = (c + 8 - p) % 8 if arriving else c
            ref = total.at[pl.ds(pl.multiple_of(core * H + at * 16, 16), 16), :]
            yield to_col(ref, ref, sems, p)

    def sum_slots(slots, n):
        value = slots[0]
        for p in range(1, n):
            value = value + slots[p]
        return value

    gram_pair.wait_recv()
    gps[0] = gpair[...] + gpart[own_rows, :]
    for copy in spread_plane(gps, gr):
        copy.start()

    def pair_copy(s):
        return to_sib(yp.at[block((y + s) % 4), other, :], yq.at[4 * s:4 * s + 4], pair, s)

    def rs_copy(s, i):
        target = 4 * ((y + s) % 4) + i
        return remote(yp.at[target, mine, :], rs.at[m], rs_sem.at[0, 4 * s + i], rs_sem.at[1, m], target * 2 + core, c)

    def scatter(s):
        pair_copy(s).wait_recv()
        for i in range(4):
            at = 4 * ((y + s) % 4) + i
            yp[at, mine, :] = yp[at, mine, :] + yq[4 * s + i]
            if s:
                rs_copy(s, i).start()
            else:
                @pl.when(x != i)
                def _():
                    rs_copy(s, i).start()

                @pl.when(x == i)
                def _():
                    rs[m] = yp[m, mine, :]

    load.wait()
    order = (2, 1, 3, 0)
    for n, s in enumerate(order):
        q = (y + s) % 4
        value = jnp.concatenate([abuf[pl.ds(4 * i + q, ROWS, stride=16), :] for i in range(4)], axis=1)
        ah, al = split(value)
        both = dot(plh[...], ah)
        value = both[0:W] + (both[W:] + dot(plh[0:W, :], al))
        for i in range(4):
            yp[4 * q + i] = value[:, i * H:(i + 1) * H]
        pair_copy(s).start()
        if n:
            scatter(order[n - 1])
    scatter(order[-1])

    for copy in spread_plane(gps, gr):
        copy.wait_recv()
    gsum[own_rows, :] = sum_slots(gps, 16)
    for copy in spread_col(gsum, ga, False):
        copy.start()

    @pl.when(is_second)
    def _():
        share_whole.wait_recv()

    @pl.when(off_source)
    def _():
        remote(own_half, own_half, px_send.at[0, 0], px_recv, sib, c).wait_recv()
        share_half.start()

    def py_copy(d, arriving):
        at = (y + 4 - d) % 4 if arriving else y
        ref = ptc.at[block(at), mine, :]
        return remote(ref, ref, py.at[0, d - 1], py.at[1, d - 1], in_plane(x, (y + d) % 4, core), c)

    for d in range(1, 4):
        py_copy(d, False).start()
    for u in range(16):
        @pl.when(m != u)
        def _():
            remote(rs.at[u], rs.at[u], rs_sem.at[0, 0], rs_sem.at[1, u], sib, c).wait_recv()
    piece = sum_slots(rs, 16)
    ytc[m, mine, :] = piece
    own = ytc.at[m, mine, :]

    @pl.when(off_source)
    def _():
        theirs = ptc.at[block(y), other, :]
        to_sib(theirs, theirs, p0).wait_recv()

    def cross_copy(p):
        rows = pl.ds(pl.multiple_of((c + p) % 8 * 16, 16), 16)
        return to_col(spart.at[rows, :], szs.at[p], sz, p)

    spart[...] = dot3(piece, ptc[m], NT)
    for p in range(1, 8):
        cross_copy(p).start()

    def z_copy(p):
        return to_col(own, yz.at[p], z_sem, p)

    def ag_copy(p, arriving):
        at = (m + 16 - p) % 16 if arriving else m
        ref = ytc.at[at, mine, :]
        return to_plane(ref, ref, ag_sem, p)

    for p in range(1, 8):
        z_copy(p).start()
    for p in range(1, 16):
        ag_copy(p, False).start()

    def x_copy(p):
        place = (c + 8 - p) % 8
        src = own if p == 0 else yz.at[p]
        return remote(src, yr.at[x, mine, :], x_sem.at[0, p], x_sem.at[1, column],
                      in_plane(place // 2, y, place % 2), c)

    def x_start(p):
        at_home = (c + 8 - p) % 8 == column

        @pl.when(at_home)
        def _():
            yr[x, mine, :] = ytc[m, mine, :] if p == 0 else yz[p]

        @pl.when(jnp.logical_not(at_home))
        def _():
            x_copy(p).start()

    x_start(0)
    for copy in spread_col(gsum, ga, True):
        copy.wait_recv()
    gram_share = to_sib(gsum.at[mine, :], gsum.at[mine, :], gs)
    gram_share.start()
    to_sib(gsum.at[other, :], gsum.at[other, :], gs).wait_recv()

    blocks = factorize(gsum, work)
    for _ in range(4):
        next(blocks)
    szs[0] = spart[pl.ds(pl.multiple_of(c * 16, 16), 16), :]
    for p in range(1, 8):
        cross_copy(p).wait_recv()
    sps[0] = sum_slots(szs, 8)
    for copy in spread_plane(sps, sr):
        copy.start()
    for _ in range(4):
        next(blocks)
    for p in range(1, 8):
        z_copy(p).wait_recv()
        x_start(p)
    for copy in spread_plane(sps, sr):
        copy.wait_recv()
    ssum[own_rows, :] = sum_slots(sps, 16)
    for copy in spread_col(ssum, sa, False):
        copy.start()

    upper = lax.broadcasted_iota(jnp.int32, (W, W), 1) >= lax.broadcasted_iota(jnp.int32, (W, W), 0)
    factor_out[...] = jnp.where(upper, work[:, :W], 0.0)
    inverse = work[:, W:]
    metric = dot(inverse, inverse, TN, HIGHEST)
    first = 2.0 * dot3(panel[...], metric)
    lhs[0:ROWS, :W], lhs[ROWS:, :W] = split(first)

    def piece_share(p, arriving):
        at = (m + 16 - p) % 16
        ref = ytc.at[at, other if arriving else mine, :]
        return to_sib(ref, ref, sib_sem, p)

    def block_share(d, arriving):
        ref = ptc.at[block((y + 4 - d) % 4), other if arriving else mine, :]
        return to_sib(ref, ref, psib, d - 1)

    piece_share(0, False).start()
    for d in range(1, 4):
        py_copy(d, True).wait_recv()
        block_share(d, False).start()
    for p in range(1, 16):
        ag_copy(p, True).wait_recv()
        piece_share(p, False).start()
    for copy in spread_col(ssum, sa, True):
        copy.wait_recv()
    cross_share = to_sib(ssum.at[mine, :], ssum.at[mine, :], ss)
    cross_share.start()
    for d in range(1, 4):
        block_share(d, True).wait_recv()
    for q in range(4):
        for i in range(4):
            lanes = pl.ds(i * H, H)
            chi[q, W:, lanes], clo[q, W:, lanes] = split(ptc[4 * q + i])
    for u in range(8):
        @pl.when(column != u)
        def _():
            ref = yr.at[u // 2, (u % 2) * H:(u % 2 + 1) * H, :]
            remote(ref, ref, x_sem.at[0, 0], x_sem.at[1, u], sib, c).wait_recv()
    image = jnp.concatenate([yr[i].T for i in range(4)], axis=0)
    for p in range(16):
        piece_share(p, True).wait_recv()
    for q in range(4):
        for i in range(4):
            lanes = pl.ds(i * H, H)
            chi[q, 0:W, lanes], clo[q, 0:W, lanes] = split(ytc[4 * q + i])
    to_sib(ssum.at[other, :], ssum.at[other, :], ss).wait_recv()
    second = 2.0 * dot3(image - dot3(first, ssum[...]), metric)
    lhs[0:ROWS, W:], lhs[ROWS:, W:] = split(second)

    for q in range(4):
        both = dot(lhs[...], chi[q])
        value = both[0:ROWS] + (both[ROWS:] + dot(lhs[0:ROWS, :], clo[q]))
        for i in range(4):
            at = pl.ds(4 * i + q, ROWS, stride=16)
            updated[at, :] = abuf[at, :] - value[:, i * H:(i + 1) * H]

    gram_pair.wait_send()
    gram_share.wait_send()
    cross_share.wait_send()

    @pl.when(is_source)
    def _():
        share_whole.wait_send()
        for d in range(1, 4):
            for k in range(2):
                px_copy(d, k).wait_send()

    @pl.when(off_source)
    def _():
        share_half.wait_send()

    for s in range(4):
        pair_copy(s).wait_send()
        for i in range(4):
            if s:
                rs_copy(s, i).wait_send()
            else:
                @pl.when(x != i)
                def _():
                    rs_copy(s, i).wait_send()

    for d in range(1, 4):
        py_copy(d, False).wait_send()
        block_share(d, False).wait_send()
    for p in range(16):
        piece_share(p, False).wait_send()
        if p:
            ag_copy(p, False).wait_send()
    for copies in (spread_plane(gps, gr), spread_col(gsum, ga, False),
                   spread_plane(sps, sr), spread_col(ssum, sa, False)):
        for copy in copies:
            copy.wait_send()
    for p in range(8):
        @pl.when((c + 8 - p) % 8 != column)
        def _():
            x_copy(p).wait_send()

        if p:
            z_copy(p).wait_send()
            cross_copy(p).wait_send()


def shards(panel, matrix):
    vmem = pltpu.VMEM
    dma = pltpu.SemaphoreType.DMA
    factor, result = pl.pallas_call(
        body,
        out_shape=(pltpu.VMEM((W, W), F32), pltpu.VMEM((ROWS * 16, H), F32)),
        in_specs=[pl.BlockSpec(memory_space=pltpu.VMEM), pl.BlockSpec(memory_space=pltpu.HBM)],
        out_specs=(pl.BlockSpec(memory_space=pltpu.VMEM), pl.BlockSpec(memory_space=pltpu.VMEM)),
        scratch_shapes=[
            vmem((ROWS * 16, H), F32), vmem((2 * W, ROWS), BF16),
            vmem((16, W, H), F32), vmem((16, H, H), F32), vmem((16, H, H), F32),
            vmem((16, W, H), F32), vmem((16, W, H), F32), vmem((8, H, H), F32), vmem((4, W, H), F32),
            vmem((4, 2 * W, ROWS), BF16), vmem((4, 2 * W, ROWS), BF16), vmem((2 * ROWS, 2 * W), BF16),
            vmem((W, W), F32), vmem((16, W), F32), vmem((16, 16, W), F32), vmem((W, W), F32),
            vmem((H, W), F32), vmem((8, 16, W), F32), vmem((16, 16, W), F32), vmem((W, W), F32),
            vmem((W, 2 * W), F32),
            dma, dma((2, 4)), dma((2, 16)), dma((2, 16)), dma((2, 16)), dma((2, 8)), dma((2, 8)),
            dma((3, 2)), dma, dma((2,)), dma((2, 3)), dma((2, 3)),
            dma((2,)), dma((2, 16)), dma((2, 8)), dma((2,)),
            dma((2, 8)), dma((2, 16)), dma((2, 8)), dma((2,)),
        ],
        compiler_params=pltpu.CompilerParams(
            collective_id=0, has_side_effects=True, vmem_limit_bytes=54 * 2**20),
        cost_estimate=pl.CostEstimate(flops=5 * 10**9, bytes_accessed=9 * 2**20, transcendentals=0),
    )(panel.reshape(ROWS, W), matrix.reshape(ROWS * 16, H))
    return factor, result.reshape(matrix.shape)


def solution(mesh):
    in_specs = (P(None, "row", None), P(None, "row", None, "col"))
    out_specs = (P(), P(None, "row", None, "col"))
    return jax.shard_map(shards, mesh=mesh, in_specs=in_specs, out_specs=out_specs, check_vma=False)
```

```python
import jax
import jax.numpy as jnp
from jax import lax
from jax.experimental import pallas as pl
from jax.experimental.pallas import tpu as pltpu
from jax.sharding import PartitionSpec as P

MESH = pl.DeviceIdType.MESH
HIGHEST = lax.Precision.HIGHEST
F32 = jnp.float32
BF16 = jnp.bfloat16
W = 256
H = 128
ROWS = 512
NB = 32

NN = (((1,), (0,)), ((), ()))
NT = (((1,), (1,)), ((), ()))
TN = (((0,), (0,)), ((), ()))


def remote(src, dst, send, recv, row, col):
    return pltpu.make_async_remote_copy(
        src_ref=src, dst_ref=dst, send_sem=send, recv_sem=recv,
        device_id={"row": row, "col": col}, device_id_type=MESH)


def split(x):
    hi = x.astype(BF16)
    return hi, (x - hi.astype(F32)).astype(BF16)


def dot(a, b, dims=NN, precision=None):
    return lax.dot_general(a, b, dims, precision=precision, preferred_element_type=F32)


def dot3(a, b, dims=NN):
    ah, al = split(a)
    bh, bl = split(b)
    return dot(ah, bh, dims) + (dot(ah, bl, dims) + dot(al, bh, dims))


def eliminate(tile):
    sub = lax.broadcasted_iota(jnp.int32, (8, 128), 0)
    groups = NB // 8
    rows = [tile[8 * g:8 * g + 8] for g in range(groups)]
    for g in range(groups):
        cols = [[jnp.broadcast_to(rows[h][:, 8 * g + k:8 * g + k + 1], (8, 128)) for h in range(g, groups)]
                for k in range(8)]
        for j in range(8):
            inverse = 1.0 / cols[j][0][j:j + 1]
            scaled = rows[g][j:j + 1] * inverse
            for k in range(j + 1, 8):
                ratio = cols[k][0][j:j + 1] * inverse
                cols[k] = [a - b * ratio for a, b in zip(cols[k], cols[j])]
            rows[g] = jnp.where(sub > j, rows[g] - cols[j][0] * scaled, rows[g])
            for h in range(g + 1, groups):
                rows[h] = rows[h] - cols[j][h - g] * scaled
    return jnp.concatenate(rows, axis=0)


def factorize(gram, work):
    lane = lax.broadcasted_iota(jnp.int32, (NB, 128), 1)
    sub = lax.broadcasted_iota(jnp.int32, (NB, 128), 0)
    eye = (lane == sub).astype(F32)
    work[...] = jnp.zeros_like(work)
    for b in range(W // NB):
        lo = b * NB
        start = lo // 128 * 128
        span = (lo + NB + 127) // 128 * 128
        unit = (lax.broadcasted_iota(jnp.int32, (NB, span), 1) ==
                lax.broadcasted_iota(jnp.int32, (NB, span), 0) + lo).astype(F32)
        rows = jnp.concatenate([gram[lo:lo + NB, start:], unit], axis=1)
        if b:
            rows = rows - dot(work[0:lo, lo:lo + NB], work[0:lo, start:W + span], TN, HIGHEST)
        square = rows[:, lo - start:lo - start + NB]
        tile = eliminate(jnp.concatenate([square, eye[:, :NB], jnp.zeros((NB, 128 - 2 * NB), F32)], axis=1))
        pivots = jnp.sum(jnp.where(lane == sub, tile, 0.0), axis=1, keepdims=True)
        inverse = tile[:, NB:2 * NB] * lax.rsqrt(pivots)
        work[lo:lo + NB, start:W + span] = dot(inverse, rows, NN, HIGHEST)
        yield


def body(panel, a_hbm, factor_out, updated,
         abuf, plh, yp, yq, rs, ytc, ptc, yz, yr, chi, clo, lhs,
         gpart, gpair, gps, gsum, spart, szs, sps, ssum, work,
         a_sem, pair, rs_sem, ag_sem, sib_sem, z_sem, x_sem,
         px_send, px_recv, p0, py, psib, gp, gr, ga, gs, sz, sr, sa, ss):
    r = lax.axis_index("row")
    c = lax.axis_index("col")
    core = r % 2
    m = r // 2
    x = m % 4
    y = m // 4
    sib = r + 1 - 2 * core
    column = 2 * x + core
    source_x = c // 2
    source_core = c % 2
    on_source = x == source_x
    is_source = r % 8 == c
    is_second = jnp.logical_and(on_source, core != source_core)
    off_source = jnp.logical_not(on_source)
    mine = pl.ds(pl.multiple_of(core * H, H), H)
    other = pl.ds(pl.multiple_of(H - core * H, H), H)

    def in_plane(xx, yy, kk):
        return (yy * 4 + xx) * 2 + kk

    load = pltpu.make_async_copy(a_hbm, abuf, a_sem)
    load.start()

    barrier = pltpu.get_barrier_semaphore()

    def greet(row, col):
        pl.semaphore_signal(barrier, inc=1, device_id={"row": row, "col": col}, device_id_type=MESH)

    greet(sib, c)
    for d in range(1, 4):
        greet(in_plane((x + d) % 4, y, 1 - core), c)
    for p in range(1, 16):
        greet(((m + p) % 16) * 2 + core, c)
    for p in range(1, 8):
        greet(r, (c + p) % 8)

    flipped = panel[...].T
    high, low = split(flipped)
    plh[0:W, :] = high
    plh[W:, :] = low
    gpart[...] = dot(flipped, flipped, NT, HIGHEST)

    @pl.when(is_source)
    def _():
        for i in range(4):
            ptc[4 * y + i] = flipped[:, i * H:(i + 1) * H]

    pl.semaphore_wait(barrier, 26)

    def to_plane(src, dst, sems, p):
        return remote(src, dst, sems.at[0, p], sems.at[1, p], ((m + p) % 16) * 2 + core, c)

    def to_col(src, dst, sems, p):
        return remote(src, dst, sems.at[0, p], sems.at[1, p], r, (c + p) % 8)

    def to_sib(src, dst, sems, *at):
        return remote(src, dst, sems.at[(0, *at)], sems.at[(1, *at)], sib, c)

    def block(q):
        return pl.ds(4 * q, 4)

    gram_pair = to_sib(gpart.at[pl.ds(pl.multiple_of(H - core * H + c * 16, 16), 16), :], gpair, gp)
    gram_pair.start()

    own_half = ptc.at[block(y), mine, :]
    whole = ptc.at[block(y), :, :]

    def px_copy(d):
        return remote(own_half, own_half, px_send.at[d - 1], px_recv, in_plane((x + d) % 4, y, core), c)

    share_whole = to_sib(whole, whole, p0)
    share_half = to_sib(own_half, own_half, p0)

    @pl.when(is_source)
    def _():
        share_whole.start()
        for d in (2, 1, 3):
            px_copy(d).start()

    own_rows = pl.ds(pl.multiple_of(core * H + c * 16, 16), 16)

    def spread_plane(slots, sems):
        for p in range(1, 16):
            yield to_plane(slots.at[0], slots.at[p], sems, p)

    def spread_col(total, sems, arriving):
        for p in range(1, 8):
            at = (c + 8 - p) % 8 if arriving else c
            ref = total.at[pl.ds(pl.multiple_of(core * H + at * 16, 16), 16), :]
            yield to_col(ref, ref, sems, p)

    def sum_slots(slots, n):
        value = slots[0]
        for p in range(1, n):
            value = value + slots[p]
        return value

    @pl.when(is_second)
    def _():
        share_whole.wait_recv()
        for d in (2, 1, 3):
            px_copy(d).start()

    gram_pair.wait_recv()
    gps[0] = gpair[...] + gpart[own_rows, :]
    for copy in spread_plane(gps, gr):
        copy.start()

    def pair_copy(s):
        return to_sib(yp.at[block((y + s) % 4), other, :], yq.at[4 * s:4 * s + 4], pair, s)

    def rs_copy(s, i):
        target = 4 * ((y + s) % 4) + i
        return remote(yp.at[target, mine, :], rs.at[m], rs_sem.at[0, 4 * s + i], rs_sem.at[1, m], target * 2 + core, c)

    def scatter(s):
        pair_copy(s).wait_recv()
        for i in range(4):
            at = 4 * ((y + s) % 4) + i
            yp[at, mine, :] = yp[at, mine, :] + yq[4 * s + i]
            if s:
                rs_copy(s, i).start()
            else:
                @pl.when(x != i)
                def _():
                    rs_copy(s, i).start()

                @pl.when(x == i)
                def _():
                    rs[m] = yp[m, mine, :]

    load.wait()
    order = (2, 1, 3, 0)
    for n, s in enumerate(order):
        q = (y + s) % 4
        value = jnp.concatenate([abuf[pl.ds(4 * i + q, ROWS, stride=16), :] for i in range(4)], axis=1)
        ah, al = split(value)
        both = dot(plh[...], ah)
        value = both[0:W] + (both[W:] + dot(plh[0:W, :], al))
        for i in range(4):
            yp[4 * q + i] = value[:, i * H:(i + 1) * H]
        pair_copy(s).start()
        if n:
            scatter(order[n - 1])
    scatter(order[-1])

    for copy in spread_plane(gps, gr):
        copy.wait_recv()
    gsum[own_rows, :] = sum_slots(gps, 16)
    for copy in spread_col(gsum, ga, False):
        copy.start()

    @pl.when(off_source)
    def _():
        px_copy(1).wait_recv()
        share_half.start()

    def py_copy(d, arriving):
        at = (y + 4 - d) % 4 if arriving else y
        ref = ptc.at[block(at), mine, :]
        return remote(ref, ref, py.at[0, d - 1], py.at[1, d - 1], in_plane(x, (y + d) % 4, core), c)

    for d in range(1, 4):
        py_copy(d, False).start()
    for u in range(16):
        @pl.when(m != u)
        def _():
            remote(rs.at[u], rs.at[u], rs_sem.at[0, 0], rs_sem.at[1, u], sib, c).wait_recv()
    piece = sum_slots(rs, 16)
    ytc[m, mine, :] = piece
    own = ytc.at[m, mine, :]

    @pl.when(off_source)
    def _():
        theirs = ptc.at[block(y), other, :]
        to_sib(theirs, theirs, p0).wait_recv()

    def cross_copy(p):
        rows = pl.ds(pl.multiple_of((c + p) % 8 * 16, 16), 16)
        return to_col(spart.at[rows, :], szs.at[p], sz, p)

    spart[...] = dot3(piece, ptc[m], NT)
    for p in range(1, 8):
        cross_copy(p).start()

    def z_copy(p):
        return to_col(own, yz.at[p], z_sem, p)

    def ag_copy(p, arriving):
        at = (m + 16 - p) % 16 if arriving else m
        ref = ytc.at[at, mine, :]
        return to_plane(ref, ref, ag_sem, p)

    for p in range(1, 8):
        z_copy(p).start()
    for p in range(1, 16):
        ag_copy(p, False).start()

    def x_copy(p):
        place = (c + 8 - p) % 8
        src = own if p == 0 else yz.at[p]
        return remote(src, yr.at[x, mine, :], x_sem.at[0, p], x_sem.at[1, column],
                      in_plane(place // 2, y, place % 2), c)

    def x_start(p):
        at_home = (c + 8 - p) % 8 == column

        @pl.when(at_home)
        def _():
            yr[x, mine, :] = ytc[m, mine, :] if p == 0 else yz[p]

        @pl.when(jnp.logical_not(at_home))
        def _():
            x_copy(p).start()

    x_start(0)
    for copy in spread_col(gsum, ga, True):
        copy.wait_recv()
    gram_share = to_sib(gsum.at[mine, :], gsum.at[mine, :], gs)
    gram_share.start()
    to_sib(gsum.at[other, :], gsum.at[other, :], gs).wait_recv()

    blocks = factorize(gsum, work)
    for _ in range(4):
        next(blocks)
    szs[0] = spart[pl.ds(pl.multiple_of(c * 16, 16), 16), :]
    for p in range(1, 8):
        cross_copy(p).wait_recv()
    sps[0] = sum_slots(szs, 8)
    for copy in spread_plane(sps, sr):
        copy.start()
    for _ in range(4):
        next(blocks)
    for p in range(1, 8):
        z_copy(p).wait_recv()
        x_start(p)
    for copy in spread_plane(sps, sr):
        copy.wait_recv()
    ssum[own_rows, :] = sum_slots(sps, 16)
    for copy in spread_col(ssum, sa, False):
        copy.start()

    upper = lax.broadcasted_iota(jnp.int32, (W, W), 1) >= lax.broadcasted_iota(jnp.int32, (W, W), 0)
    factor_out[...] = jnp.where(upper, work[:, :W], 0.0)
    inverse = work[:, W:]
    metric = dot(inverse, inverse, TN, HIGHEST)
    first = 2.0 * dot3(panel[...], metric)
    lhs[0:ROWS, :W], lhs[ROWS:, :W] = split(first)

    def piece_share(p, arriving):
        at = (m + 16 - p) % 16
        ref = ytc.at[at, other if arriving else mine, :]
        return to_sib(ref, ref, sib_sem, p)

    def block_share(d, arriving):
        ref = ptc.at[block((y + 4 - d) % 4), other if arriving else mine, :]
        return to_sib(ref, ref, psib, d - 1)

    piece_share(0, False).start()
    for d in range(1, 4):
        py_copy(d, True).wait_recv()
        block_share(d, False).start()
    for p in range(1, 16):
        ag_copy(p, True).wait_recv()
        piece_share(p, False).start()
    for copy in spread_col(ssum, sa, True):
        copy.wait_recv()
    cross_share = to_sib(ssum.at[mine, :], ssum.at[mine, :], ss)
    cross_share.start()
    for d in range(1, 4):
        block_share(d, True).wait_recv()
    for q in range(4):
        for i in range(4):
            lanes = pl.ds(i * H, H)
            chi[q, W:, lanes], clo[q, W:, lanes] = split(ptc[4 * q + i])
    for u in range(8):
        @pl.when(column != u)
        def _():
            ref = yr.at[u // 2, (u % 2) * H:(u % 2 + 1) * H, :]
            remote(ref, ref, x_sem.at[0, 0], x_sem.at[1, u], sib, c).wait_recv()
    image = jnp.concatenate([yr[i].T for i in range(4)], axis=0)
    for p in range(16):
        piece_share(p, True).wait_recv()
    for q in range(4):
        for i in range(4):
            lanes = pl.ds(i * H, H)
            chi[q, 0:W, lanes], clo[q, 0:W, lanes] = split(ytc[4 * q + i])
    to_sib(ssum.at[other, :], ssum.at[other, :], ss).wait_recv()
    second = 2.0 * dot3(image - dot3(first, ssum[...]), metric)
    lhs[0:ROWS, W:], lhs[ROWS:, W:] = split(second)

    for q in range(4):
        both = dot(lhs[...], chi[q])
        value = both[0:ROWS] + (both[ROWS:] + dot(lhs[0:ROWS, :], clo[q]))
        for i in range(4):
            at = pl.ds(4 * i + q, ROWS, stride=16)
            updated[at, :] = abuf[at, :] - value[:, i * H:(i + 1) * H]

    gram_pair.wait_send()
    gram_share.wait_send()
    cross_share.wait_send()

    @pl.when(is_source)
    def _():
        share_whole.wait_send()

    @pl.when(on_source)
    def _():
        for d in range(1, 4):
            px_copy(d).wait_send()

    @pl.when(off_source)
    def _():
        share_half.wait_send()

    for s in range(4):
        pair_copy(s).wait_send()
        for i in range(4):
            if s:
                rs_copy(s, i).wait_send()
            else:
                @pl.when(x != i)
                def _():
                    rs_copy(s, i).wait_send()

    for d in range(1, 4):
        py_copy(d, False).wait_send()
        block_share(d, False).wait_send()
    for p in range(16):
        piece_share(p, False).wait_send()
        if p:
            ag_copy(p, False).wait_send()
    for copies in (spread_plane(gps, gr), spread_col(gsum, ga, False),
                   spread_plane(sps, sr), spread_col(ssum, sa, False)):
        for copy in copies:
            copy.wait_send()
    for p in range(8):
        @pl.when((c + 8 - p) % 8 != column)
        def _():
            x_copy(p).wait_send()

        if p:
            z_copy(p).wait_send()
            cross_copy(p).wait_send()


def shards(panel, matrix):
    vmem = pltpu.VMEM
    dma = pltpu.SemaphoreType.DMA
    factor, result = pl.pallas_call(
        body,
        out_shape=(pltpu.VMEM((W, W), F32), pltpu.VMEM((ROWS * 16, H), F32)),
        in_specs=[pl.BlockSpec(memory_space=pltpu.VMEM), pl.BlockSpec(memory_space=pltpu.HBM)],
        out_specs=(pl.BlockSpec(memory_space=pltpu.VMEM), pl.BlockSpec(memory_space=pltpu.VMEM)),
        scratch_shapes=[
            vmem((ROWS * 16, H), F32), vmem((2 * W, ROWS), BF16),
            vmem((16, W, H), F32), vmem((16, H, H), F32), vmem((16, H, H), F32),
            vmem((16, W, H), F32), vmem((16, W, H), F32), vmem((8, H, H), F32), vmem((4, W, H), F32),
            vmem((4, 2 * W, ROWS), BF16), vmem((4, 2 * W, ROWS), BF16), vmem((2 * ROWS, 2 * W), BF16),
            vmem((W, W), F32), vmem((16, W), F32), vmem((16, 16, W), F32), vmem((W, W), F32),
            vmem((H, W), F32), vmem((8, 16, W), F32), vmem((16, 16, W), F32), vmem((W, W), F32),
            vmem((W, 2 * W), F32),
            dma, dma((2, 4)), dma((2, 16)), dma((2, 16)), dma((2, 16)), dma((2, 8)), dma((2, 8)),
            dma((3,)), dma, dma((2,)), dma((2, 3)), dma((2, 3)),
            dma((2,)), dma((2, 16)), dma((2, 8)), dma((2,)),
            dma((2, 8)), dma((2, 16)), dma((2, 8)), dma((2,)),
        ],
        compiler_params=pltpu.CompilerParams(
            collective_id=0, has_side_effects=True, vmem_limit_bytes=54 * 2**20),
        cost_estimate=pl.CostEstimate(flops=5 * 10**9, bytes_accessed=9 * 2**20, transcendentals=0),
    )(panel.reshape(ROWS, W), matrix.reshape(ROWS * 16, H))
    return factor, result.reshape(matrix.shape)


def solution(mesh):
    in_specs = (P(None, "row", None), P(None, "row", None, "col"))
    out_specs = (P(), P(None, "row", None, "col"))
    return jax.shard_map(shards, mesh=mesh, in_specs=in_specs, out_specs=out_specs, check_vma=False)
```

```python
import jax
import jax.numpy as jnp
from jax import lax
from jax.experimental import pallas as pl
from jax.experimental.pallas import tpu as pltpu
from jax.sharding import PartitionSpec as P

MESH = pl.DeviceIdType.MESH
HIGHEST = lax.Precision.HIGHEST
F32 = jnp.float32
BF16 = jnp.bfloat16
W = 256
H = 128
ROWS = 512
NB = 32

NN = (((1,), (0,)), ((), ()))
NT = (((1,), (1,)), ((), ()))
TN = (((0,), (0,)), ((), ()))


def remote(src, dst, send, recv, row, col):
    return pltpu.make_async_remote_copy(
        src_ref=src, dst_ref=dst, send_sem=send, recv_sem=recv,
        device_id={"row": row, "col": col}, device_id_type=MESH)


def split(x):
    hi = x.astype(BF16)
    return hi, (x - hi.astype(F32)).astype(BF16)


def dot(a, b, dims=NN, precision=None):
    return lax.dot_general(a, b, dims, precision=precision, preferred_element_type=F32)


def dot3(a, b, dims=NN):
    ah, al = split(a)
    bh, bl = split(b)
    return dot(ah, bh, dims) + (dot(ah, bl, dims) + dot(al, bh, dims))


def eliminate(tile):
    sub = lax.broadcasted_iota(jnp.int32, (8, 128), 0)
    groups = NB // 8
    rows = [tile[8 * g:8 * g + 8] for g in range(groups)]
    for g in range(groups):
        cols = [[jnp.broadcast_to(rows[h][:, 8 * g + k:8 * g + k + 1], (8, 128)) for h in range(g, groups)]
                for k in range(8)]
        for j in range(8):
            inverse = 1.0 / cols[j][0][j:j + 1]
            scaled = rows[g][j:j + 1] * inverse
            for k in range(j + 1, 8):
                ratio = cols[k][0][j:j + 1] * inverse
                cols[k] = [a - b * ratio for a, b in zip(cols[k], cols[j])]
            rows[g] = jnp.where(sub > j, rows[g] - cols[j][0] * scaled, rows[g])
            for h in range(g + 1, groups):
                rows[h] = rows[h] - cols[j][h - g] * scaled
    return jnp.concatenate(rows, axis=0)


def factorize(gram, work):
    lane = lax.broadcasted_iota(jnp.int32, (NB, 128), 1)
    sub = lax.broadcasted_iota(jnp.int32, (NB, 128), 0)
    eye = (lane == sub).astype(F32)
    work[...] = jnp.zeros_like(work)
    for b in range(W // NB):
        lo = b * NB
        start = lo // 128 * 128
        span = (lo + NB + 127) // 128 * 128
        unit = (lax.broadcasted_iota(jnp.int32, (NB, span), 1) ==
                lax.broadcasted_iota(jnp.int32, (NB, span), 0) + lo).astype(F32)
        rows = jnp.concatenate([gram[lo:lo + NB, start:], unit], axis=1)
        if b:
            rows = rows - dot(work[0:lo, lo:lo + NB], work[0:lo, start:W + span], TN, HIGHEST)
        square = rows[:, lo - start:lo - start + NB]
        tile = eliminate(jnp.concatenate([square, eye[:, :NB], jnp.zeros((NB, 128 - 2 * NB), F32)], axis=1))
        pivots = jnp.sum(jnp.where(lane == sub, tile, 0.0), axis=1, keepdims=True)
        inverse = tile[:, NB:2 * NB] * lax.rsqrt(pivots)
        work[lo:lo + NB, start:W + span] = dot(inverse, rows, NN, HIGHEST)
        yield


def body(panel, a_hbm, factor_out, updated,
         abuf, plh, yp, yq, rs, ytc, ptc, yz, yr, chi, clo, lhs,
         gpart, gpair, gps, gsum, spart, szs, sps, ssum, work,
         a_sem, pair, rs_sem, ag_sem, sib_sem, z_sem, x_sem,
         px_send, px_recv, p0, py, psib, gp, gr, ga, gs, sz, sr, sa, ss):
    r = lax.axis_index("row")
    c = lax.axis_index("col")
    core = r % 2
    m = r // 2
    x = m % 4
    y = m // 4
    sib = r + 1 - 2 * core
    column = 2 * x + core
    source_x = c // 2
    source_core = c % 2
    on_source = x == source_x
    is_source = r % 8 == c
    is_second = jnp.logical_and(on_source, core != source_core)
    off_source = jnp.logical_not(on_source)
    mine = pl.ds(pl.multiple_of(core * H, H), H)
    other = pl.ds(pl.multiple_of(H - core * H, H), H)

    def in_plane(xx, yy, kk):
        return (yy * 4 + xx) * 2 + kk

    load = pltpu.make_async_copy(a_hbm, abuf, a_sem)
    load.start()

    barrier = pltpu.get_barrier_semaphore()

    def greet(row, col):
        pl.semaphore_signal(barrier, inc=1, device_id={"row": row, "col": col}, device_id_type=MESH)

    greet(sib, c)
    for d in range(1, 4):
        greet(in_plane((x + d) % 4, y, 1 - core), c)
    for p in range(1, 16):
        greet(((m + p) % 16) * 2 + core, c)
    for p in range(1, 8):
        greet(r, (c + p) % 8)

    flipped = panel[...].T
    high, low = split(flipped)
    plh[0:W, :] = high
    plh[W:, :] = low
    gpart[...] = dot(flipped, flipped, NT, HIGHEST)

    @pl.when(is_source)
    def _():
        for i in range(4):
            ptc[4 * y + i] = flipped[:, i * H:(i + 1) * H]

    pl.semaphore_wait(barrier, 26)

    def to_plane(src, dst, sems, p):
        return remote(src, dst, sems.at[0, p], sems.at[1, p], ((m + p) % 16) * 2 + core, c)

    def to_col(src, dst, sems, p):
        return remote(src, dst, sems.at[0, p], sems.at[1, p], r, (c + p) % 8)

    def to_sib(src, dst, sems, *at):
        return remote(src, dst, sems.at[(0, *at)], sems.at[(1, *at)], sib, c)

    def block(q):
        return pl.ds(4 * q, 4)

    gram_pair = to_sib(gpart.at[pl.ds(pl.multiple_of(H - core * H + c * 16, 16), 16), :], gpair, gp)
    gram_pair.start()

    own_half = ptc.at[block(y), mine, :]
    whole = ptc.at[block(y), :, :]

    def px_copy(d):
        return remote(own_half, own_half, px_send.at[d - 1], px_recv, in_plane((x + d) % 4, y, core), c)

    share_whole = to_sib(whole, whole, p0)
    share_half = to_sib(own_half, own_half, p0)

    @pl.when(is_source)
    def _():
        share_whole.start()
        for d in (2, 1, 3):
            px_copy(d).start()

    own_rows = pl.ds(pl.multiple_of(core * H + c * 16, 16), 16)

    def spread_plane(slots, sems):
        for p in range(1, 16):
            yield to_plane(slots.at[0], slots.at[p], sems, p)

    def spread_col(total, sems, arriving):
        for p in range(1, 8):
            at = (c + 8 - p) % 8 if arriving else c
            ref = total.at[pl.ds(pl.multiple_of(core * H + at * 16, 16), 16), :]
            yield to_col(ref, ref, sems, p)

    def sum_slots(slots, n):
        value = slots[0]
        for p in range(1, n):
            value = value + slots[p]
        return value

    @pl.when(is_second)
    def _():
        share_whole.wait_recv()
        for d in (2, 1, 3):
            px_copy(d).start()

    gram_pair.wait_recv()
    gps[0] = gpair[...] + gpart[own_rows, :]
    for copy in spread_plane(gps, gr):
        copy.start()

    def pair_copy(s):
        return to_sib(yp.at[block((y + s) % 4), other, :], yq.at[4 * s:4 * s + 4], pair, s)

    def rs_copy(s, i):
        target = 4 * ((y + s) % 4) + i
        return remote(yp.at[target, mine, :], rs.at[m], rs_sem.at[0, 4 * s + i], rs_sem.at[1, m], target * 2 + core, c)

    def scatter(s):
        pair_copy(s).wait_recv()
        for i in range(4):
            at = 4 * ((y + s) % 4) + i
            yp[at, mine, :] = yp[at, mine, :] + yq[4 * s + i]
            if s:
                rs_copy(s, i).start()
            else:
                @pl.when(x != i)
                def _():
                    rs_copy(s, i).start()

                @pl.when(x == i)
                def _():
                    rs[m] = yp[m, mine, :]

    load.wait()
    order = (2, 1, 3, 0)
    for n, s in enumerate(order):
        q = (y + s) % 4
        value = jnp.concatenate([abuf[pl.ds(4 * i + q, ROWS, stride=16), :] for i in range(4)], axis=1)
        ah, al = split(value)
        both = dot(plh[...], ah)
        value = both[0:W] + (both[W:] + dot(plh[0:W, :], al))
        for i in range(4):
            yp[4 * q + i] = value[:, i * H:(i + 1) * H]
        pair_copy(s).start()
        if n:
            scatter(order[n - 1])
    scatter(order[-1])

    @pl.when(off_source)
    def _():
        px_copy(1).wait_recv()
        share_half.start()

    def py_copy(d, arriving):
        at = (y + 4 - d) % 4 if arriving else y
        ref = ptc.at[block(at), mine, :]
        return remote(ref, ref, py.at[0, d - 1], py.at[1, d - 1], in_plane(x, (y + d) % 4, core), c)

    for d in range(1, 4):
        py_copy(d, False).start()

    for copy in spread_plane(gps, gr):
        copy.wait_recv()
    gsum[own_rows, :] = sum_slots(gps, 16)
    for copy in spread_col(gsum, ga, False):
        copy.start()
    for u in range(16):
        @pl.when(m != u)
        def _():
            remote(rs.at[u], rs.at[u], rs_sem.at[0, 0], rs_sem.at[1, u], sib, c).wait_recv()
    piece = sum_slots(rs, 16)
    ytc[m, mine, :] = piece
    own = ytc.at[m, mine, :]

    @pl.when(off_source)
    def _():
        theirs = ptc.at[block(y), other, :]
        to_sib(theirs, theirs, p0).wait_recv()

    def cross_copy(p):
        rows = pl.ds(pl.multiple_of((c + p) % 8 * 16, 16), 16)
        return to_col(spart.at[rows, :], szs.at[p], sz, p)

    spart[...] = dot3(piece, ptc[m], NT)
    for p in range(1, 8):
        cross_copy(p).start()

    def z_copy(p):
        return to_col(own, yz.at[p], z_sem, p)

    def ag_copy(p, arriving):
        at = (m + 16 - p) % 16 if arriving else m
        ref = ytc.at[at, mine, :]
        return to_plane(ref, ref, ag_sem, p)

    for p in range(1, 8):
        z_copy(p).start()
    for p in range(1, 16):
        ag_copy(p, False).start()

    def x_copy(p):
        place = (c + 8 - p) % 8
        src = own if p == 0 else yz.at[p]
        return remote(src, yr.at[x, mine, :], x_sem.at[0, p], x_sem.at[1, column],
                      in_plane(place // 2, y, place % 2), c)

    def x_start(p):
        at_home = (c + 8 - p) % 8 == column

        @pl.when(at_home)
        def _():
            yr[x, mine, :] = ytc[m, mine, :] if p == 0 else yz[p]

        @pl.when(jnp.logical_not(at_home))
        def _():
            x_copy(p).start()

    x_start(0)
    for copy in spread_col(gsum, ga, True):
        copy.wait_recv()
    gram_share = to_sib(gsum.at[mine, :], gsum.at[mine, :], gs)
    gram_share.start()
    to_sib(gsum.at[other, :], gsum.at[other, :], gs).wait_recv()

    blocks = factorize(gsum, work)
    for _ in range(4):
        next(blocks)
    szs[0] = spart[pl.ds(pl.multiple_of(c * 16, 16), 16), :]
    for p in range(1, 8):
        cross_copy(p).wait_recv()
    sps[0] = sum_slots(szs, 8)
    for copy in spread_plane(sps, sr):
        copy.start()
    for _ in range(4):
        next(blocks)
    for p in range(1, 8):
        z_copy(p).wait_recv()
        x_start(p)
    for copy in spread_plane(sps, sr):
        copy.wait_recv()
    ssum[own_rows, :] = sum_slots(sps, 16)
    for copy in spread_col(ssum, sa, False):
        copy.start()

    upper = lax.broadcasted_iota(jnp.int32, (W, W), 1) >= lax.broadcasted_iota(jnp.int32, (W, W), 0)
    factor_out[...] = jnp.where(upper, work[:, :W], 0.0)
    inverse = work[:, W:]
    metric = dot(inverse, inverse, TN, HIGHEST)
    first = 2.0 * dot3(panel[...], metric)
    lhs[0:ROWS, :W], lhs[ROWS:, :W] = split(first)

    def piece_share(p, arriving):
        at = (m + 16 - p) % 16
        ref = ytc.at[at, other if arriving else mine, :]
        return to_sib(ref, ref, sib_sem, p)

    def block_share(d, arriving):
        ref = ptc.at[block((y + 4 - d) % 4), other if arriving else mine, :]
        return to_sib(ref, ref, psib, d - 1)

    piece_share(0, False).start()
    for d in range(1, 4):
        py_copy(d, True).wait_recv()
        block_share(d, False).start()
    for p in range(1, 16):
        ag_copy(p, True).wait_recv()
        piece_share(p, False).start()
    for copy in spread_col(ssum, sa, True):
        copy.wait_recv()
    cross_share = to_sib(ssum.at[mine, :], ssum.at[mine, :], ss)
    cross_share.start()
    for d in range(1, 4):
        block_share(d, True).wait_recv()
    for q in range(4):
        for i in range(4):
            lanes = pl.ds(i * H, H)
            chi[q, W:, lanes], clo[q, W:, lanes] = split(ptc[4 * q + i])
    for u in range(8):
        @pl.when(column != u)
        def _():
            ref = yr.at[u // 2, (u % 2) * H:(u % 2 + 1) * H, :]
            remote(ref, ref, x_sem.at[0, 0], x_sem.at[1, u], sib, c).wait_recv()
    image = jnp.concatenate([yr[i].T for i in range(4)], axis=0)
    for p in range(16):
        piece_share(p, True).wait_recv()
    for q in range(4):
        for i in range(4):
            lanes = pl.ds(i * H, H)
            chi[q, 0:W, lanes], clo[q, 0:W, lanes] = split(ytc[4 * q + i])
    to_sib(ssum.at[other, :], ssum.at[other, :], ss).wait_recv()
    second = 2.0 * dot3(image - dot3(first, ssum[...]), metric)
    lhs[0:ROWS, W:], lhs[ROWS:, W:] = split(second)

    for q in range(4):
        both = dot(lhs[...], chi[q])
        value = both[0:ROWS] + (both[ROWS:] + dot(lhs[0:ROWS, :], clo[q]))
        for i in range(4):
            at = pl.ds(4 * i + q, ROWS, stride=16)
            updated[at, :] = abuf[at, :] - value[:, i * H:(i + 1) * H]

    gram_pair.wait_send()
    gram_share.wait_send()
    cross_share.wait_send()

    @pl.when(is_source)
    def _():
        share_whole.wait_send()

    @pl.when(on_source)
    def _():
        for d in range(1, 4):
            px_copy(d).wait_send()

    @pl.when(off_source)
    def _():
        share_half.wait_send()

    for s in range(4):
        pair_copy(s).wait_send()
        for i in range(4):
            if s:
                rs_copy(s, i).wait_send()
            else:
                @pl.when(x != i)
                def _():
                    rs_copy(s, i).wait_send()

    for d in range(1, 4):
        py_copy(d, False).wait_send()
        block_share(d, False).wait_send()
    for p in range(16):
        piece_share(p, False).wait_send()
        if p:
            ag_copy(p, False).wait_send()
    for copies in (spread_plane(gps, gr), spread_col(gsum, ga, False),
                   spread_plane(sps, sr), spread_col(ssum, sa, False)):
        for copy in copies:
            copy.wait_send()
    for p in range(8):
        @pl.when((c + 8 - p) % 8 != column)
        def _():
            x_copy(p).wait_send()

        if p:
            z_copy(p).wait_send()
            cross_copy(p).wait_send()


def shards(panel, matrix):
    vmem = pltpu.VMEM
    dma = pltpu.SemaphoreType.DMA
    factor, result = pl.pallas_call(
        body,
        out_shape=(pltpu.VMEM((W, W), F32), pltpu.VMEM((ROWS * 16, H), F32)),
        in_specs=[pl.BlockSpec(memory_space=pltpu.VMEM), pl.BlockSpec(memory_space=pltpu.HBM)],
        out_specs=(pl.BlockSpec(memory_space=pltpu.VMEM), pl.BlockSpec(memory_space=pltpu.VMEM)),
        scratch_shapes=[
            vmem((ROWS * 16, H), F32), vmem((2 * W, ROWS), BF16),
            vmem((16, W, H), F32), vmem((16, H, H), F32), vmem((16, H, H), F32),
            vmem((16, W, H), F32), vmem((16, W, H), F32), vmem((8, H, H), F32), vmem((4, W, H), F32),
            vmem((4, 2 * W, ROWS), BF16), vmem((4, 2 * W, ROWS), BF16), vmem((2 * ROWS, 2 * W), BF16),
            vmem((W, W), F32), vmem((16, W), F32), vmem((16, 16, W), F32), vmem((W, W), F32),
            vmem((H, W), F32), vmem((8, 16, W), F32), vmem((16, 16, W), F32), vmem((W, W), F32),
            vmem((W, 2 * W), F32),
            dma, dma((2, 4)), dma((2, 16)), dma((2, 16)), dma((2, 16)), dma((2, 8)), dma((2, 8)),
            dma((3,)), dma, dma((2,)), dma((2, 3)), dma((2, 3)),
            dma((2,)), dma((2, 16)), dma((2, 8)), dma((2,)),
            dma((2, 8)), dma((2, 16)), dma((2, 8)), dma((2,)),
        ],
        compiler_params=pltpu.CompilerParams(
            collective_id=0, has_side_effects=True, vmem_limit_bytes=54 * 2**20),
        cost_estimate=pl.CostEstimate(flops=5 * 10**9, bytes_accessed=9 * 2**20, transcendentals=0),
    )(panel.reshape(ROWS, W), matrix.reshape(ROWS * 16, H))
    return factor, result.reshape(matrix.shape)


def solution(mesh):
    in_specs = (P(None, "row", None), P(None, "row", None, "col"))
    out_specs = (P(), P(None, "row", None, "col"))
    return jax.shard_map(shards, mesh=mesh, in_specs=in_specs, out_specs=out_specs, check_vma=False)
```
